256 devices in a mesh: tm: 128 (over y_lo, z, x, core), mode: 2 (over y_hi).
Axes of the slice: x: 4, y: 4 (y_hi: 2, y_lo: 2; y = y_hi * 2 + y_lo), z: 8, core: 2. Of those that a mesh axis runs over, the one named last changes fastest.
Arguments:
- elementals: bfloat16 [128, 128, 128, 128], P('tm', 'mode'), may hold values from -6 to 6
- slice_scale: float32 [128], P('tm'), may hold values from 0.5 to 2
- source_times: int32 [512, 1], replicated, may hold values from 0 to 127; in each aligned block of 512 rows (0 to 511, 512 to 1023, ...) at most 8 rows name the same one
- perambulators: bfloat16 [128, 8, 2, 128, 128], P('tm'), may hold values from -0.5 to 0.5
Outputs:
- correlator: float32 [128, 8, 2], P('tm')
The draws below stay inside these ranges and needn't reach their ends.
Inputs may be any that keep to these rules, and one draw needn't show every extreme that they name: `source_times`: each of the 512 entries is a source time; no time is listed more than 8 times and some time is listed exactly 8 times; every time is listed at least once.
All inputs are finite; a program needn't handle non-finite values.
Results may differ from the reference program's by a relative error of at most 0.011.
Values may be sent and summed in bfloat16 or wider, within the bound.
A program may use at most 64 MiB of HBM per device.

```python
import math
import jax
import jax.numpy as jnp
import numpy as np
from jax import lax

M = 128
NT = 128
CAP = 8
NSOLVE = 512


def levels(own_key, dims, cuts, low, high):
    gain = 1.0
    for position, parts in cuts:
        heights = jax.random.uniform(jax.random.fold_in(jax.random.fold_in(own_key, 6), position), (parts,), jnp.float32, low / len(cuts), high / len(cuts))
        gain = gain * jnp.repeat(jnp.exp(heights), dims[position] // parts).reshape((-1,) + (1,) * (len(dims) - 1 - position))
    return gain


def deal_out(key, own, number, rows, count, top, limit, slope):
    order = jax.random.permutation(key, count)
    packed, common = portions_of(count, rows * top, limit, slope, True), portions_of(count, rows * top, limit, slope, False)
    places = jnp.arange(count)

    def named(sizes, rotation):
        used = int((sizes > 0).sum())
        fixed = max(1, used // 4)
        passed = fixed + (places - fixed + rotation * (used - fixed)) % max(1, count - fixed)
        return jnp.zeros((count,), jnp.int32).at[order[jnp.where(places < fixed, places, passed)]].set(jnp.asarray(sizes, jnp.int32))

    sizes = jnp.where(number % 4 == 0, named(packed, number // 4), named(common, number - number // 4 - 1))
    mixed = jax.random.permutation(jax.random.fold_in(own, 3), count)
    giver, taker = mixed[0:count // 2 * 2:2], mixed[1:count // 2 * 2:2]
    room = jnp.minimum(sizes[giver] - 1, limit - sizes[taker]) // 2
    room = jnp.where((giver == order[0]) | (taker == order[0]) | (sizes[taker] == 0), 0, jnp.maximum(room, 0))
    passed = jax.random.randint(jax.random.fold_in(own, 4), (count // 2,), 0, 1 << 20) % (room + 1)
    sizes = sizes.at[giver].add(-passed).at[taker].add(passed)
    members = jnp.searchsorted(jnp.cumsum(sizes), jnp.arange(rows * top), side="right").astype(jnp.int32)
    table = members.reshape(top, rows).T
    table = table[jax.random.permutation(jax.random.fold_in(own, 1), rows)]
    rotation = jax.random.randint(jax.random.fold_in(own, 2), (rows, 1), 0, top)
    return jnp.take_along_axis(table, (jnp.arange(top)[None, :] + rotation) % top, axis=1)


def portions_of(count, total, reach, skew, full):
    loads = [(1 << 20) // math.isqrt(grade ** skew) + 1 for grade in range(1, count + 1)]
    largest = reach if full else min(reach, max(-(-total // count), total * loads[0] // sum(loads)))
    least = 1 if total - largest >= count - 1 else 0
    holding, surplus = [largest] + [least] * (count - 1), total - largest - least * (count - 1)
    while surplus > 0:
        free = [i for i in range(1, count) if holding[i] < largest] or [i for i in range(1, count) if holding[i] < reach]
        mass, budget = sum([loads[i] for i in free]), surplus
        for i in free:
            extra = min(reach - holding[i], max(1, budget * loads[i] // mass), surplus)
            holding[i] = holding[i] + extra
            surplus = surplus - extra
    return np.array(holding)


def scatter_about(stream_key, extent, spread, most, cuts=(), held_as=jnp.bfloat16):
    entries = spread * jax.random.normal(stream_key, extent, jnp.float32)
    if cuts:
        entries = entries * levels(stream_key, extent, cuts, -0.22, 0.18)
    return jnp.clip(entries, -most, most).astype(held_as)


def setup_inputs(seed: int = 0) -> dict:
    key_list = jax.random.split(jax.random.key(seed), 5)
    elementals = scatter_about(key_list[0], (NT, M, M, M), 1.0, 6.0, ((0, 128), (1, 2)))
    slice_scale = jnp.clip(jnp.exp(math.log(2.0) - 1.3862944 * jax.random.uniform(key_list[1], (NT,), jnp.float32) ** levels(key_list[1], (NT,), ((0, 128),), -0.2, 0.2)), 0.5, 2.0)
    source_times_keys = jax.random.split(jax.random.fold_in(key_list[2], 1), NSOLVE // NSOLVE)
    source_times_turns = jax.random.permutation(jax.random.fold_in(key_list[2], 3), NSOLVE // NSOLVE)
    source_times = jax.vmap(lambda own, number: deal_out(jax.random.fold_in(key_list[2], 2), own, number, NSOLVE, NT, 1, CAP, 2))(source_times_keys, source_times_turns).reshape((NSOLVE, 1))
    perambulators = scatter_about(key_list[3], (NT, CAP, 2, M, M), M ** -0.5, 0.5, ((0, 128),))
    return dict(elementals=elementals, slice_scale=slice_scale, source_times=source_times, perambulators=perambulators)


def source_image(source, peram_block):
    mode_width = source.shape[0]
    first_pass = jnp.dot(source.reshape(mode_width * mode_width, mode_width), peram_block.T, preferred_element_type=jnp.float32)
    first_pass = first_pass.astype(jnp.bfloat16).reshape(source.shape)
    second_pass = jnp.einsum('bq,pqc->pbc', peram_block.astype(jnp.float32), first_pass.astype(jnp.float32))
    return second_pass.astype(jnp.bfloat16)

def reference(elementals, slice_scale, source_times, perambulators):
    listed = source_times[:, 0]
    moments = jnp.arange(NT, dtype=jnp.int32)
    counts = lax.optimization_barrier(jnp.sum((listed[None, :] == moments[:, None]).astype(jnp.int32), axis=1))
    factor = 1.0 / (M * math.sqrt(M))

    def one_entry(flat_index):
        source_time = flat_index // (CAP * 2)
        slot_index = flat_index // 2 % CAP
        offset = flat_index % 2 + 1
        sink_time = (source_time + offset) % NT
        parity = jnp.where(source_time + offset >= NT, -1.0, 1.0).astype(jnp.float32)
        peram_block = perambulators[source_time, slot_index, offset - 1]

        def compute(unused):
            image_full = source_image(elementals[source_time], peram_block)
            pair_sums = jnp.einsum('abc,pbc->ap', elementals[sink_time].astype(jnp.float32), image_full.astype(jnp.float32))
            total = jnp.sum(peram_block.astype(jnp.float32) * pair_sums)
            return (total * parity * slice_scale[source_time] * slice_scale[sink_time] * factor).astype(jnp.float32)

        def empty_entry(unused):
            return jnp.zeros((), jnp.float32)
        return lax.cond(slot_index < counts[source_time], compute, empty_entry, 0)
    values = lax.map(one_entry, jnp.arange(NT * CAP * 2, dtype=jnp.int32))
    return values.reshape(NT, CAP, 2)
```

```python
import functools
import math

import jax
import jax.numpy as jnp
from jax import lax
from jax.experimental import pallas as pl
from jax.experimental.pallas import tpu as pltpu
from jax.sharding import PartitionSpec as P

MESH = pl.DeviceIdType.MESH
F32, BF16 = jnp.float32, jnp.bfloat16
CHUNK = 16
PIECES = 2


def kernel(
    elem, scale, listed, peram, out,
    x_own, x_peer, x_rows, y_raw, y_cols, blocks, left, right, first, moved, acc,
    scale_own, scale_far, part, far,
    own_sem, peram_sem, x_send, x_recv, y_send, y_recv, p_send, p_recv, s_send, s_recv, o_send, o_recv,
):
    slices = lax.axis_size("tm")
    t, h = lax.axis_index("tm"), lax.axis_index("mode")
    core = lax.rem(t, 2)
    half, modes = elem.shape[1], elem.shape[2]
    slots = peram.shape[1]
    chunks, span = modes // CHUNK, half // PIECES
    other = 1 - h

    def at(step):
        return lax.rem(t + step + slices, slices)

    def send(src, dst, ssem, rsem, device):
        return pltpu.make_async_remote_copy(
            src_ref=src, dst_ref=dst, send_sem=ssem, recv_sem=rsem, device_id=device, device_id_type=MESH
        )

    def x_copy(i):
        rows = pl.ds(i * CHUNK, CHUNK)
        return send(elem.at[0, :, rows, :], x_peer.at[i], x_send.at[i], x_recv.at[i], (t, other))

    def y_copy(j, q, device):
        rows = pl.ds(q * span, span)
        return send(elem.at[0, rows], y_raw.at[j, rows], y_send.at[j, q], y_recv.at[j, q], device)

    def forward(q):
        rows = pl.ds(q * span, span)
        return send(y_raw.at[1, rows], y_raw.at[0, rows], y_send.at[0, q], y_recv.at[0, q], (at(1), h))

    def peram_copy():
        return send(peram.at[0, :, 1], blocks.at[1], p_send, p_recv, (at(2), h))

    def scale_copy(d):
        return send(scale_own, scale_far.at[d], s_send.at[d], s_recv.at[d], (at(-1 - d), h))

    own_copy = pltpu.make_async_copy(elem.at[0], x_own, own_sem)
    own_copy.start()
    block_copies = [pltpu.make_async_copy(peram.at[0, :, d], blocks.at[d], peram_sem.at[d]) for d in range(2)]
    block_copies[0].start()

    @pl.when(core == 0)
    def _():
        block_copies[1].start()

    scale_own[...] = jnp.full(scale_own.shape, scale[0], F32)
    acc[...] = jnp.zeros_like(acc)

    barrier = pltpu.get_barrier_semaphore()
    near = [(t, other)] + [(at(k), h) for k in (-2, -1, 1, 2)] + [(at(k), other) for k in (-2, 2)]
    for device in near:
        pl.semaphore_signal(barrier, inc=1, device_id=device, device_id_type=MESH)
    pl.semaphore_wait(barrier, len(near))

    @pl.when(core == 1)
    def _():
        peram_copy().start()
        for q in range(PIECES):
            y_copy(1, q, (at(2), h)).start()
            y_copy(0, q, (at(-1), h)).start()

    @pl.when(core == 0)
    def _():
        for q in range(PIECES):
            y_copy(1, q, (at(-2), h)).start()

    for d in range(2):
        scale_copy(d).start()
    for i in range(chunks):
        x_copy(i).start()

    block_copies[0].wait()

    @pl.when(core == 0)
    def _():
        block_copies[1].wait()

    @pl.when(core == 1)
    def _():
        peram_copy().wait_recv()

    right[...] = jnp.zeros_like(right)
    own_rows = pl.multiple_of(h * half, half)
    for j in range(2):
        swap = (core == 1) & (j == 1)

        def lay_block(r, _):
            block = blocks[j, r]
            turned = block.T
            row_form = jnp.where(swap, turned, block) if j else block
            column_form = jnp.where(swap, block, turned) if j else turned
            blocks[j, r] = row_form
            for q in range(PIECES):
                rows = pl.ds(pl.multiple_of(j * slots * span + r * span, span), span)
                left[q, rows, :] = blocks[j, r, pl.ds(own_rows + q * span, span), :]
            right[j * slots + r, :modes, :modes] = column_form
            right[j * slots + r, modes:, modes:] = column_form
            return 0

        lax.fori_loop(0, slots, lay_block, 0)

    def lay_rows(chunk_rows, i, offset):
        turned = jnp.swapaxes(chunk_rows.astype(F32), 0, 1).astype(BF16)
        for p in range(CHUNK // 2):
            pair = jnp.concatenate([turned[p], turned[p + CHUNK // 2]], axis=1)
            x_rows[i * (CHUNK // 2) + p, pl.ds(offset, half), :] = pair

    own_copy.wait()

    def lay_own(i, _):
        rows = pl.ds(pl.multiple_of(i * CHUNK, CHUNK), CHUNK)
        lay_rows(x_own[:, rows, :], i, own_rows)
        return 0

    lax.fori_loop(0, chunks, lay_own, 0)

    def take_piece(q):
        @pl.when(core == 0)
        def _():
            y_copy(1, q, (at(2), h)).wait_recv()
            forward(q).start()
            y_copy(0, q, (at(-1), h)).wait_recv()

        @pl.when(core == 1)
        def _():
            y_copy(1, q, (at(2), h)).wait_recv()
            forward(q).wait_recv()

        def lay(n, _):
            j, y = n // span, lax.rem(n, span)
            rows = pl.ds(pl.multiple_of(y * modes, modes), modes)
            y_cols[j, q, rows, :] = y_raw[j, q * span + y].T
            return 0

        lax.fori_loop(0, 2 * span, lay, 0)

    early = chunks // 2

    def unit(n, _):
        late = n - 2 * early
        i = jnp.where(n < 2 * early, lax.rem(n, early), early + late // 2)
        q = jnp.where(n < 2 * early, n // early, lax.rem(late, 2))

        @pl.when(n == 0)
        def _():
            take_piece(0)

        @pl.when(n == early)
        def _():
            take_piece(1)

        @pl.when((n < early) | ((late >= 0) & (q == 0)))
        def _():
            x_copy(i).wait_recv()
            lay_rows(x_peer[i], i, pl.multiple_of(other * half, half))

        for p in range(CHUNK // 2):
            product = jnp.dot(left[q], x_rows[i * (CHUNK // 2) + p], preferred_element_type=F32)
            first[p] = product.astype(BF16)
        for j in range(2):
            for r in range(slots):
                lo = (j * slots + r) * span
                lhs = first[:, lo:lo + span, :].reshape(CHUNK // 2 * span, 2 * modes)
                image = jnp.dot(lhs, right[j * slots + r], preferred_element_type=F32)
                turned = jnp.swapaxes(image.reshape(CHUNK // 2, span, 2 * modes), 0, 1)
                for y in range(span):
                    tile = jnp.concatenate([turned[y, :, :modes], turned[y, :, modes:]], axis=0)
                    moved[j, r * CHUNK:(r + 1) * CHUNK, y * modes:(y + 1) * modes] = tile.astype(BF16)
        rows = pl.ds(pl.multiple_of(i * CHUNK, CHUNK), CHUNK)
        for j in range(2):
            sums = jnp.dot(moved[j], y_cols[j, q], preferred_element_type=F32)
            weights = right[pl.ds(j * slots, slots), rows, :modes].reshape(slots * CHUNK, modes)
            acc[j] += sums * weights.astype(F32)
        return 0

    lax.fori_loop(0, 2 * chunks, unit, 0)

    for j in range(2):
        total = jnp.sum(acc[j].reshape(slots, CHUNK, modes), axis=1)
        part[j] = jnp.broadcast_to(jnp.sum(total, axis=1, keepdims=True), (slots, modes))

    def part_copy(j, slot, device):
        return send(part.at[j], far.at[slot], o_send.at[slot], o_recv.at[slot], device)

    part_copy(0, 0, (t, other)).start()

    @pl.when(core == 0)
    def _():
        part_copy(1, 2, (t, other)).start()
        far[1] = part[1]

    @pl.when(core == 1)
    def _():
        part_copy(1, 1, (at(-2), h)).start()
        part_copy(1, 2, (at(-2), other)).start()

    live = jnp.sum((listed[...] == t).astype(jnp.int32))
    slot_of = lax.broadcasted_iota(jnp.int32, (slots, modes), 0)
    lane = lax.broadcasted_iota(jnp.int32, (slots, modes), 1)
    for d in range(2):
        scale_copy(d).wait_recv()
    factor = 1.0 / (modes * math.sqrt(modes))
    signs = [jnp.where(t + d >= slices, -factor, factor) for d in (1, 2)]
    weights = jnp.where(lane == 0, scale_far[0] * signs[0], scale_far[1] * signs[1]) * scale_own[...]

    part_copy(0, 0, (t, other)).wait_recv()
    part_copy(1, 2, (t, other)).wait_recv()

    @pl.when(core == 1)
    def _():
        part_copy(1, 1, (at(-2), h)).wait_recv()

    values = jnp.where(lane == 0, part[0] + far[0], far[1] + far[2]) * weights
    values = jnp.where(slot_of < live, values, 0.0)
    out[0] = values[:, :2]

    part_copy(0, 0, (t, other)).wait_send()
    part_copy(1, 2, (t, other)).wait_send()

    @pl.when(core == 0)
    def _():
        for q in range(PIECES):
            y_copy(1, q, (at(-2), h)).wait_send()
            forward(q).wait_send()

    @pl.when(core == 1)
    def _():
        peram_copy().wait_send()
        part_copy(1, 1, (at(-2), h)).wait_send()
        for q in range(PIECES):
            y_copy(1, q, (at(2), h)).wait_send()
            y_copy(0, q, (at(-1), h)).wait_send()

    for d in range(2):
        scale_copy(d).wait_send()
    for i in range(chunks):
        x_copy(i).wait_send()


def local(elementals, slice_scale, source_times, perambulators):
    half, modes = elementals.shape[1:3]
    slots = perambulators.shape[1]
    chunks, span = modes // CHUNK, half // PIECES
    dma, in_hbm = pltpu.SemaphoreType.DMA, pl.BlockSpec(memory_space=pltpu.HBM)
    return pl.pallas_call(
        kernel,
        out_shape=jax.ShapeDtypeStruct((1, slots, 2), F32),
        in_specs=[
            in_hbm,
            pl.BlockSpec(memory_space=pltpu.SMEM),
            pl.BlockSpec(memory_space=pltpu.VMEM),
            in_hbm,
        ],
        out_specs=pl.BlockSpec(memory_space=pltpu.VMEM),
        scratch_shapes=[
            pltpu.VMEM((half, modes, modes), BF16),
            pltpu.VMEM((chunks, half, CHUNK, modes), BF16),
            pltpu.VMEM((modes // 2, 2 * half, 2 * modes), BF16),
            pltpu.VMEM((2, half, modes, modes), BF16),
            pltpu.VMEM((2, PIECES, span * modes, modes), BF16),
            pltpu.VMEM((2, slots, modes, modes), BF16),
            pltpu.VMEM((PIECES, 2 * slots * span, modes), BF16),
            pltpu.VMEM((2 * slots, 2 * modes, 2 * modes), BF16),
            pltpu.VMEM((CHUNK // 2, 2 * slots * span, 2 * modes), BF16),
            pltpu.VMEM((2, slots * CHUNK, span * modes), BF16),
            pltpu.VMEM((2, slots * CHUNK, modes), F32),
            pltpu.VMEM((slots, modes), F32),
            pltpu.VMEM((2, slots, modes), F32),
            pltpu.VMEM((2, slots, modes), F32),
            pltpu.VMEM((3, slots, modes), F32),
            dma, dma((2,)),
            dma((chunks,)), dma((chunks,)),
            dma((2, PIECES)), dma((2, PIECES)),
            dma, dma,
            dma((2,)), dma((2,)),
            dma((3,)), dma((3,)),
        ],
        compiler_params=pltpu.CompilerParams(
            collective_id=0, has_side_effects=True, vmem_limit_bytes=48 * 2**20
        ),
    )(elementals, slice_scale, source_times.T, perambulators)


def solution(mesh):
    in_specs = (P("tm", "mode", None, None), P("tm"), P(), P("tm", None, None, None, None))
    return jax.shard_map(
        local, mesh=mesh, in_specs=in_specs, out_specs=P("tm", None, None), check_vma=False
    )
```

```python
import functools
import math

import jax
import jax.numpy as jnp
from jax import lax
from jax.experimental import pallas as pl
from jax.experimental.pallas import tpu as pltpu
from jax.sharding import PartitionSpec as P

MESH = pl.DeviceIdType.MESH
F32, BF16 = jnp.float32, jnp.bfloat16
CHUNK = 16
PIECES = 2
STRIDE = 8


def kernel(
    elem, scale, listed, peram, out,
    x_own, x_peer, x_rows, y_raw, blocks, left, right, first, moved, acc,
    scale_own, scale_far, part, far, passing,
    own_sem, peram_sem, x_send, x_recv, y_send, y_recv, p_send, p_recv, s_send, s_recv, o_send, o_recv, r_send, r_recv,
):
    slices = lax.axis_size("tm")
    t, h = lax.axis_index("tm"), lax.axis_index("mode")
    core = lax.rem(t, 2)
    half, modes = elem.shape[1], elem.shape[2]
    slots = peram.shape[1]
    chunks, span = modes // CHUNK, half // PIECES
    other = 1 - h

    def at(step):
        return lax.rem(t + step + slices, slices)

    def send(src, dst, ssem, rsem, device):
        return pltpu.make_async_remote_copy(
            src_ref=src, dst_ref=dst, send_sem=ssem, recv_sem=rsem, device_id=device, device_id_type=MESH
        )

    def x_copy(i):
        rows = pl.ds(i * CHUNK, CHUNK)
        return send(elem.at[0, :, rows, :], x_peer.at[i], x_send.at[i], x_recv.at[i], (t, other))

    def y_copy(j, q, device):
        rows = pl.ds(q * span, span)
        return send(elem.at[0, rows], y_raw.at[j, rows], y_send.at[j, q], y_recv.at[j, q], device)

    def forward(q):
        rows = pl.ds(q * span, span)
        return send(y_raw.at[1, rows], y_raw.at[0, rows], y_send.at[0, q], y_recv.at[0, q], (at(1), h))

    def peram_copy():
        return send(peram.at[0, :, 1], blocks.at[1], p_send, p_recv, (at(2), h))

    def scale_copy(d):
        return send(scale_own, scale_far.at[d], s_send.at[d], s_recv.at[d], (at(-1 - d), h))

    run = slices // 2
    place, upper = lax.rem(t, run), t // run
    relays = run // STRIDE
    share = span // relays
    rank = place // STRIDE
    lead = jnp.where(core == 1, 1, STRIDE - 2)
    at_source = place == jnp.where(core == 1, run - 1, 0)
    at_sink = place == jnp.where(core == 1, 1, run - 2)
    is_relay = (lax.rem(place, STRIDE) == lead) & jnp.logical_not(at_sink)
    sink = upper * run + jnp.where(core == 1, 1, run - 2)
    source = lax.rem(sink + jnp.where(core == 1, slices - 2, 2), slices)
    ahead = lax.rem(t + jnp.where(core == 1, 2, slices - 2), slices)

    def share_rows(q, k):
        return pl.ds(q * span + k * share, share)

    def share_copy(q, k, dst, rsem, device):
        return send(elem.at[0, share_rows(q, k)], dst, y_send.at[1, q], rsem, device)

    def pass_on(q):
        return send(passing.at[q], y_raw.at[1, share_rows(q, rank)], r_send.at[q], y_recv.at[1, q], (sink, h))

    own_copy = pltpu.make_async_copy(elem.at[0], x_own, own_sem)
    own_copy.start()
    block_copies = [pltpu.make_async_copy(peram.at[0, :, d], blocks.at[d], peram_sem.at[d]) for d in range(2)]
    block_copies[0].start()

    @pl.when(core == 0)
    def _():
        block_copies[1].start()

    scale_own[...] = jnp.full(scale_own.shape, scale[0], F32)
    acc[...] = jnp.zeros_like(acc)

    barrier = pltpu.get_barrier_semaphore()
    near = [(t, other)] + [(at(k), h) for k in (-2, -1, 1, 2)] + [(at(k), other) for k in (-2, 2)]
    for device in near:
        pl.semaphore_signal(barrier, inc=1, device_id=device, device_id_type=MESH)

    @pl.when(is_relay)
    def _():
        pl.semaphore_signal(barrier, inc=1, device_id=(source, h), device_id_type=MESH)

    @pl.when(at_sink)
    def _():
        def greet(k, _):
            @pl.when(k != rank)
            def _():
                relay = upper * run + k * STRIDE + lead
                pl.semaphore_signal(barrier, inc=1, device_id=(relay, h), device_id_type=MESH)

            return 0

        lax.fori_loop(0, relays, greet, 0)

    further = jnp.where(is_relay, 1, 0) + jnp.where(at_source, relays - 1, 0)
    pl.semaphore_wait(barrier, len(near) + further)

    @pl.when(core == 1)
    def _():
        peram_copy().start()

    @pl.when(at_source)
    def _():
        def spread(n, _):
            q, k = n // relays, lax.rem(n, relays)
            relay = (1 - upper) * run + k * STRIDE + lead

            @pl.when(relay == ahead)
            def _():
                share_copy(q, k, y_raw.at[1, share_rows(q, k)], y_recv.at[1, q], (relay, h)).start()

            @pl.when(relay != ahead)
            def _():
                share_copy(q, k, passing.at[q], r_recv.at[q], (relay, h)).start()

            return 0

        lax.fori_loop(0, PIECES * relays, spread, 0)

    @pl.when(jnp.logical_not(at_source))
    def _():
        for q in range(PIECES):
            y_copy(1, q, (ahead, h)).start()

    @pl.when(core == 1)
    def _():
        for q in range(PIECES):
            y_copy(0, q, (at(-1), h)).start()

    for d in range(2):
        scale_copy(d).start()
    for i in range(chunks):
        x_copy(i).start()

    right[...] = jnp.zeros_like(right)
    own_rows = pl.multiple_of(h * half, half)

    def lay_blocks(j):
        swap = (core == 1) & (j == 1)

        def lay_block(r, _):
            block = blocks[j, r]
            turned = block.T
            row_form = jnp.where(swap, turned, block) if j else block
            column_form = jnp.where(swap, block, turned) if j else turned
            blocks[j, r] = row_form
            for q in range(PIECES):
                rows = pl.ds(pl.multiple_of(r * span, span), span)
                left[j, q, rows, :] = blocks[j, r, pl.ds(own_rows + q * span, span), :]
            right[j * slots + r, :modes, :modes] = column_form
            right[j * slots + r, modes:, modes:] = column_form
            return 0

        lax.fori_loop(0, slots, lay_block, 0)

    def lay_rows(chunk_rows, i, offset):
        turned = jnp.swapaxes(chunk_rows.astype(F32), 0, 1).astype(BF16)
        for p in range(CHUNK // 2):
            pair = jnp.concatenate([turned[p], turned[p + CHUNK // 2]], axis=1)
            x_rows[i * (CHUNK // 2) + p, pl.ds(offset, half), :] = pair

    def lay_own(i, _):
        rows = pl.ds(pl.multiple_of(i * CHUNK, CHUNK), CHUNK)
        lay_rows(x_own[:, rows, :], i, own_rows)
        return 0

    block_copies[0].wait()
    lay_blocks(0)
    own_copy.wait()
    lax.fori_loop(0, chunks, lay_own, 0)

    @pl.when(core == 0)
    def _():
        block_copies[1].wait()

    @pl.when(core == 1)
    def _():
        peram_copy().wait_recv()

    lay_blocks(1)

    def take(q):
        y_copy(1, q, (at(2), h)).wait_recv()

        @pl.when(core == 0)
        def _():
            forward(q).start()

        @pl.when(is_relay)
        def _():
            share_copy(q, 0, passing.at[q], r_recv.at[q], (source, h)).wait_recv()
            pass_on(q).start()

        y_copy(0, q, (at(-1), h)).wait_recv()

    early = chunks // 2

    def unit(n, _):
        late = n - 2 * early
        i = jnp.where(n < 2 * early, lax.rem(n, early), early + late // 2)
        q = jnp.where(n < 2 * early, n // early, lax.rem(late, 2))

        for piece in range(PIECES):
            @pl.when(n == piece * early)
            def _():
                take(piece)

        @pl.when((n < early) | ((late >= 0) & (q == 0)))
        def _():
            x_copy(i).wait_recv()
            lay_rows(x_peer[i], i, pl.multiple_of(other * half, half))

        for j in range(2):
            for p in range(CHUNK // 2):
                product = jnp.dot(left[j, q], x_rows[i * (CHUNK // 2) + p], preferred_element_type=F32)
                first[j, p] = product.astype(BF16)
        for j in range(2):
            for r in range(slots):
                lhs = first[j, :, r * span:(r + 1) * span, :].reshape(CHUNK // 2 * span, 2 * modes)
                image = jnp.dot(lhs, right[j * slots + r], preferred_element_type=F32)
                turned = jnp.swapaxes(image.reshape(CHUNK // 2, span, 2 * modes), 0, 1)
                for y in range(span):
                    tile = jnp.concatenate([turned[y, :, :modes], turned[y, :, modes:]], axis=0)
                    moved[j, r * CHUNK:(r + 1) * CHUNK, y * modes:(y + 1) * modes] = tile.astype(BF16)
        rows = pl.ds(pl.multiple_of(i * CHUNK, CHUNK), CHUNK)
        for j in range(2):
            sink_rows = jnp.concatenate([y_raw[j, q * span + y] for y in range(span)], axis=1)
            sums = lax.dot_general(moved[j], sink_rows, (((1,), (1,)), ((), ())), preferred_element_type=F32)
            weights = right[j * slots:(j + 1) * slots, rows, :modes].reshape(slots * CHUNK, modes)
            acc[j] += sums * weights.astype(F32)
        return 0

    lax.fori_loop(0, 2 * chunks, unit, 0)

    for j in range(2):
        total = jnp.sum(acc[j].reshape(slots, CHUNK, modes), axis=1)
        part[j] = jnp.broadcast_to(jnp.sum(total, axis=1, keepdims=True), (slots, modes))

    def part_copy(j, slot, device):
        return send(part.at[j], far.at[slot], o_send.at[slot], o_recv.at[slot], device)

    part_copy(0, 0, (t, other)).start()

    @pl.when(core == 0)
    def _():
        part_copy(1, 2, (t, other)).start()
        far[1] = part[1]

    @pl.when(core == 1)
    def _():
        part_copy(1, 1, (at(-2), h)).start()
        part_copy(1, 2, (at(-2), other)).start()

    live = jnp.sum((listed[...] == t).astype(jnp.int32))
    slot_of = lax.broadcasted_iota(jnp.int32, (slots, modes), 0)
    lane = lax.broadcasted_iota(jnp.int32, (slots, modes), 1)
    for d in range(2):
        scale_copy(d).wait_recv()
    factor = 1.0 / (modes * math.sqrt(modes))
    signs = [jnp.where(t + d >= slices, -factor, factor) for d in (1, 2)]
    weights = jnp.where(lane == 0, scale_far[0] * signs[0], scale_far[1] * signs[1]) * scale_own[...]

    part_copy(0, 0, (t, other)).wait_recv()
    part_copy(1, 2, (t, other)).wait_recv()

    @pl.when(core == 1)
    def _():
        part_copy(1, 1, (at(-2), h)).wait_recv()

    values = jnp.where(lane == 0, part[0] + far[0], far[1] + far[2]) * weights
    values = jnp.where(slot_of < live, values, 0.0)
    out[0] = values[:, :2]

    part_copy(0, 0, (t, other)).wait_send()
    part_copy(1, 2, (t, other)).wait_send()

    for q in range(PIECES):
        y_copy(1, q, (ahead, h)).wait_send()

    @pl.when(core == 0)
    def _():
        for q in range(PIECES):
            forward(q).wait_send()

    @pl.when(core == 1)
    def _():
        peram_copy().wait_send()
        part_copy(1, 1, (at(-2), h)).wait_send()
        for q in range(PIECES):
            y_copy(0, q, (at(-1), h)).wait_send()

    @pl.when(is_relay)
    def _():
        for q in range(PIECES):
            pass_on(q).wait_send()

    for d in range(2):
        scale_copy(d).wait_send()
    for i in range(chunks):
        x_copy(i).wait_send()


def local(elementals, slice_scale, source_times, perambulators):
    half, modes = elementals.shape[1:3]
    slots = perambulators.shape[1]
    chunks, span = modes // CHUNK, half // PIECES
    dma, in_hbm = pltpu.SemaphoreType.DMA, pl.BlockSpec(memory_space=pltpu.HBM)
    return pl.pallas_call(
        kernel,
        out_shape=jax.ShapeDtypeStruct((1, slots, 2), F32),
        in_specs=[
            in_hbm,
            pl.BlockSpec(memory_space=pltpu.SMEM),
            pl.BlockSpec(memory_space=pltpu.VMEM),
            in_hbm,
        ],
        out_specs=pl.BlockSpec(memory_space=pltpu.VMEM),
        scratch_shapes=[
            pltpu.VMEM((half, modes, modes), BF16),
            pltpu.VMEM((chunks, half, CHUNK, modes), BF16),
            pltpu.VMEM((modes // 2, 2 * half, 2 * modes), BF16),
            pltpu.VMEM((2, half, modes, modes), BF16),
            pltpu.VMEM((2, slots, modes, modes), BF16),
            pltpu.VMEM((2, PIECES, slots * span, modes), BF16),
            pltpu.VMEM((2 * slots, 2 * modes, 2 * modes), BF16),
            pltpu.VMEM((2, CHUNK // 2, slots * span, 2 * modes), BF16),
            pltpu.VMEM((2, slots * CHUNK, span * modes), BF16),
            pltpu.VMEM((2, slots * CHUNK, modes), F32),
            pltpu.VMEM((slots, modes), F32),
            pltpu.VMEM((2, slots, modes), F32),
            pltpu.VMEM((2, slots, modes), F32),
            pltpu.VMEM((3, slots, modes), F32),
            pltpu.VMEM((PIECES, span * STRIDE * 2 // lax.axis_size("tm"), modes, modes), BF16),
            dma, dma((2,)),
            dma((chunks,)), dma((chunks,)),
            dma((2, PIECES)), dma((2, PIECES)),
            dma, dma,
            dma((2,)), dma((2,)),
            dma((3,)), dma((3,)),
            dma((PIECES,)), dma((PIECES,)),
        ],
        compiler_params=pltpu.CompilerParams(
            collective_id=0, has_side_effects=True, vmem_limit_bytes=60 * 2**20
        ),
    )(elementals, slice_scale, source_times.T, perambulators)


def solution(mesh):
    in_specs = (P("tm", "mode", None, None), P("tm"), P(), P("tm", None, None, None, None))
    return jax.shard_map(
        local, mesh=mesh, in_specs=in_specs, out_specs=P("tm", None, None), check_vma=False
    )
```

```python
import functools
import math

import jax
import jax.numpy as jnp
from jax import lax
from jax.experimental import pallas as pl
from jax.experimental.pallas import tpu as pltpu
from jax.sharding import PartitionSpec as P

MESH = pl.DeviceIdType.MESH
F32, BF16 = jnp.float32, jnp.bfloat16
CHUNK = 16
PIECES = 2
STRIDE = 8


def kernel(
    elem, scale, listed, peram, out,
    x_own, x_peer, x_rows, y_raw, blocks, left, right, first, moved, acc,
    scale_own, scale_far, part, far, passing,
    own_sem, peram_sem, x_send, x_recv, y_send, y_recv, p_send, p_recv, s_send, s_recv, o_send, o_recv, r_send, r_recv,
):
    slices = lax.axis_size("tm")
    t, h = lax.axis_index("tm"), lax.axis_index("mode")
    core = lax.rem(t, 2)
    half, modes = elem.shape[1], elem.shape[2]
    slots = peram.shape[1]
    chunks, span = modes // CHUNK, half // PIECES
    other = 1 - h

    def at(step):
        return lax.rem(t + step + slices, slices)

    def send(src, dst, ssem, rsem, device):
        return pltpu.make_async_remote_copy(
            src_ref=src, dst_ref=dst, send_sem=ssem, recv_sem=rsem, device_id=device, device_id_type=MESH
        )

    def x_copy(i):
        rows = pl.ds(i * CHUNK, CHUNK)
        return send(elem.at[0, :, rows, :], x_peer.at[i], x_send.at[i], x_recv.at[i], (t, other))

    def y_copy(j, q, device):
        rows = pl.ds(q * span, span)
        return send(elem.at[0, rows], y_raw.at[j, rows], y_send.at[j, q], y_recv.at[j, q], device)

    def forward(q):
        rows = pl.ds(q * span, span)
        return send(y_raw.at[1, rows], y_raw.at[0, rows], y_send.at[0, q], y_recv.at[0, q], (at(1), h))

    def peram_copy():
        return send(peram.at[0, :, 1], blocks.at[1], p_send, p_recv, (at(2), h))

    def scale_copy(d):
        return send(scale_own, scale_far.at[d], s_send.at[d], s_recv.at[d], (at(-1 - d), h))

    run = slices // 2
    place, upper = lax.rem(t, run), t // run
    relays = run // STRIDE
    share = span // relays
    rank = place // STRIDE
    leads = [jnp.where(core == 1, 1 + 2 * q, STRIDE - 2 - 2 * q) for q in range(PIECES)]
    at_source = place == jnp.where(core == 1, run - 1, 0)
    at_sink = place == jnp.where(core == 1, 1, run - 2)
    relays_piece = [(lax.rem(place, STRIDE) == lead) & jnp.logical_not(at_sink) for lead in leads]
    sink = upper * run + jnp.where(core == 1, 1, run - 2)
    source = lax.rem(sink + jnp.where(core == 1, slices - 2, 2), slices)
    ahead = lax.rem(t + jnp.where(core == 1, 2, slices - 2), slices)

    def share_rows(q, k):
        return pl.ds(q * span + k * share, share)

    def share_copy(q, k, dst, rsem, device):
        return send(elem.at[0, share_rows(q, k)], dst, y_send.at[1, q], rsem, device)

    def pass_on(q):
        return send(passing.at[q], y_raw.at[1, share_rows(q, rank)], r_send.at[q], y_recv.at[1, q], (sink, h))

    own_copy = pltpu.make_async_copy(elem.at[0], x_own, own_sem)
    own_copy.start()
    block_copies = [pltpu.make_async_copy(peram.at[0, :, d], blocks.at[d], peram_sem.at[d]) for d in range(2)]
    block_copies[0].start()

    @pl.when(core == 0)
    def _():
        block_copies[1].start()

    scale_own[...] = jnp.full(scale_own.shape, scale[0], F32)
    acc[...] = jnp.zeros_like(acc)

    barrier = pltpu.get_barrier_semaphore()
    near = [(t, other)] + [(at(k), h) for k in (-2, -1, 1, 2)] + [(at(k), other) for k in (-2, 2)]
    for device in near:
        pl.semaphore_signal(barrier, inc=1, device_id=device, device_id_type=MESH)

    @pl.when(relays_piece[0] | relays_piece[1])
    def _():
        pl.semaphore_signal(barrier, inc=1, device_id=(source, h), device_id_type=MESH)

    @pl.when(at_sink)
    def _():
        def greet(n, _):
            relay = upper * run + lax.rem(n, relays) * STRIDE + jnp.where(n < relays, leads[0], leads[1])

            @pl.when(relay != t)
            def _():
                pl.semaphore_signal(barrier, inc=1, device_id=(relay, h), device_id_type=MESH)

            return 0

        lax.fori_loop(0, PIECES * relays, greet, 0)

    further = jnp.where(relays_piece[0] | relays_piece[1], 1, 0) + jnp.where(at_source, PIECES * relays - 1, 0)
    pl.semaphore_wait(barrier, len(near) + further)

    for i in range(2):
        x_copy(i).start()

    @pl.when(core == 1)
    def _():
        peram_copy().start()

    @pl.when(at_source)
    def _():
        def spread(n, _):
            q, k = n // relays, lax.rem(n, relays)
            relay = (1 - upper) * run + k * STRIDE + jnp.where(q == 0, leads[0], leads[1])

            @pl.when(relay == ahead)
            def _():
                share_copy(q, k, y_raw.at[1, share_rows(q, k)], y_recv.at[1, q], (relay, h)).start()

            @pl.when(relay != ahead)
            def _():
                share_copy(q, k, passing.at[q], r_recv.at[q], (relay, h)).start()

            return 0

        group = relays // 2
        for g in range(2 * PIECES):
            lax.fori_loop(g * group, (g + 1) * group, spread, 0)
            x_copy(2 + g).start()

    @pl.when(jnp.logical_not(at_source))
    def _():
        for q in range(PIECES):
            y_copy(1, q, (ahead, h)).start()
        for g in range(2 * PIECES):
            x_copy(2 + g).start()

    @pl.when(core == 1)
    def _():
        for q in range(PIECES):
            y_copy(0, q, (at(-1), h)).start()

    for i in range(2 + 2 * PIECES, chunks):
        x_copy(i).start()
    for d in range(2):
        scale_copy(d).start()

    right[...] = jnp.zeros_like(right)
    own_rows = pl.multiple_of(h * half, half)

    def lay_blocks(j):
        swap = (core == 1) & (j == 1)

        def lay_block(r, _):
            block = blocks[j, r]
            turned = block.T
            row_form = jnp.where(swap, turned, block) if j else block
            column_form = jnp.where(swap, block, turned) if j else turned
            blocks[j, r] = row_form
            for q in range(PIECES):
                rows = pl.ds(pl.multiple_of(r * span, span), span)
                left[j, q, rows, :] = blocks[j, r, pl.ds(own_rows + q * span, span), :]
            right[j * slots + r, :modes, :modes] = column_form
            right[j * slots + r, modes:, modes:] = column_form
            return 0

        lax.fori_loop(0, slots, lay_block, 0)

    def lay_rows(chunk_rows, i, offset):
        turned = jnp.swapaxes(chunk_rows.astype(F32), 0, 1).astype(BF16)
        for p in range(CHUNK // 2):
            pair = jnp.concatenate([turned[p], turned[p + CHUNK // 2]], axis=1)
            x_rows[i * (CHUNK // 2) + p, pl.ds(offset, half), :] = pair

    def lay_own(i, _):
        rows = pl.ds(pl.multiple_of(i * CHUNK, CHUNK), CHUNK)
        lay_rows(x_own[:, rows, :], i, own_rows)
        return 0

    block_copies[0].wait()
    lay_blocks(0)
    own_copy.wait()
    lax.fori_loop(0, chunks, lay_own, 0)

    @pl.when(core == 0)
    def _():
        block_copies[1].wait()

    @pl.when(core == 1)
    def _():
        peram_copy().wait_recv()

    lay_blocks(1)

    def take_near(q):
        y_copy(0, q, (at(-1), h)).wait_recv()

    def take_far(q):
        y_copy(1, q, (at(2), h)).wait_recv()

        @pl.when(core == 0)
        def _():
            forward(q).start()

    def relay(q):
        @pl.when(relays_piece[q])
        def _():
            share_copy(q, 0, passing.at[q], r_recv.at[q], (source, h)).wait_recv()
            pass_on(q).start()

    def take_chunk(i):
        x_copy(i).wait_recv()
        lay_rows(x_peer[i], i, pl.multiple_of(other * half, half))

    near_late = (core == 1) & at_source
    far_late = (core == 1) & at_sink
    early = chunks // 2
    last = PIECES - 1

    def step(n, _):
        @pl.when(n == 0)
        def _():
            take_chunk(0)
            relay(0)
            take_far(0)
            take_near(0)
            take_chunk(1)

        @pl.when(n == 1)
        def _():
            take_chunk(2)
            relay(last)
            take_chunk(3)

        far_at = jnp.where(at_sink, jnp.where(core == 1, 3, 2), 1)

        @pl.when(n == far_at)
        def _():
            take_far(last)

        @pl.when(n == jnp.where(near_late, 3, 2))
        def _():
            take_near(last)

        @pl.when(n >= early)
        def _():
            take_chunk(n)

        pairs, apart = n < early, (near_late | far_late) & ((n == 2) | (n == 3))
        late_first = (n == 2) == near_late
        blocks_of = []
        for b in range(4):
            c = jnp.where(pairs, 2 * lax.rem(n, 2) + b // 2, n)
            q = jnp.where(pairs, n // 2, b // 2)
            c = jnp.where(apart, b, c)
            j = jnp.where(apart, jnp.where(late_first, 1, 0), b % 2)
            blocks_of.append((c, j, q))
        for b, (c, j, q) in enumerate(blocks_of):
            for p in range(CHUNK // 2):
                product = jnp.dot(left[j, q], x_rows[c * (CHUNK // 2) + p], preferred_element_type=F32)
                first[b, p] = product.astype(BF16)
        for b, (c, j, q) in enumerate(blocks_of):
            for r in range(slots):
                lhs = first[b, :, r * span:(r + 1) * span, :].reshape(CHUNK // 2 * span, 2 * modes)
                image = jnp.dot(lhs, right[j * slots + r], preferred_element_type=F32)
                turned = jnp.swapaxes(image.reshape(CHUNK // 2, span, 2 * modes), 0, 1)
                for y in range(span):
                    tile = jnp.concatenate([turned[y, :, :modes], turned[y, :, modes:]], axis=0)
                    moved[b, r * CHUNK:(r + 1) * CHUNK, y * modes:(y + 1) * modes] = tile.astype(BF16)
        for b, (c, j, q) in enumerate(blocks_of):
            rows = pl.ds(pl.multiple_of(c * CHUNK, CHUNK), CHUNK)
            sink_rows = jnp.concatenate([y_raw[j, q * span + y] for y in range(span)], axis=1)
            sums = lax.dot_general(moved[b], sink_rows, (((1,), (1,)), ((), ())), preferred_element_type=F32)
            weights = right[pl.ds(j * slots, slots), rows, :modes].reshape(slots * CHUNK, modes)
            acc[j] += sums * weights.astype(F32)
        return 0

    lax.fori_loop(0, chunks, step, 0)

    for j in range(2):
        total = jnp.sum(acc[j].reshape(slots, CHUNK, modes), axis=1)
        part[j] = jnp.broadcast_to(jnp.sum(total, axis=1, keepdims=True), (slots, modes))

    def part_copy(j, slot, device):
        return send(part.at[j], far.at[slot], o_send.at[slot], o_recv.at[slot], device)

    part_copy(0, 0, (t, other)).start()

    @pl.when(core == 0)
    def _():
        part_copy(1, 2, (t, other)).start()
        far[1] = part[1]

    @pl.when(core == 1)
    def _():
        part_copy(1, 1, (at(-2), h)).start()
        part_copy(1, 2, (at(-2), other)).start()

    live = jnp.sum((listed[...] == t).astype(jnp.int32))
    slot_of = lax.broadcasted_iota(jnp.int32, (slots, modes), 0)
    lane = lax.broadcasted_iota(jnp.int32, (slots, modes), 1)
    for d in range(2):
        scale_copy(d).wait_recv()
    factor = 1.0 / (modes * math.sqrt(modes))
    signs = [jnp.where(t + d >= slices, -factor, factor) for d in (1, 2)]
    weights = jnp.where(lane == 0, scale_far[0] * signs[0], scale_far[1] * signs[1]) * scale_own[...]

    part_copy(0, 0, (t, other)).wait_recv()
    part_copy(1, 2, (t, other)).wait_recv()

    @pl.when(core == 1)
    def _():
        part_copy(1, 1, (at(-2), h)).wait_recv()

    values = jnp.where(lane == 0, part[0] + far[0], far[1] + far[2]) * weights
    values = jnp.where(slot_of < live, values, 0.0)
    out[0] = values[:, :2]

    part_copy(0, 0, (t, other)).wait_send()
    part_copy(1, 2, (t, other)).wait_send()

    for q in range(PIECES):
        y_copy(1, q, (ahead, h)).wait_send()

    @pl.when(core == 0)
    def _():
        for q in range(PIECES):
            forward(q).wait_send()

    @pl.when(core == 1)
    def _():
        peram_copy().wait_send()
        part_copy(1, 1, (at(-2), h)).wait_send()
        for q in range(PIECES):
            y_copy(0, q, (at(-1), h)).wait_send()

    for q in range(PIECES):
        @pl.when(relays_piece[q])
        def _():
            pass_on(q).wait_send()

    for d in range(2):
        scale_copy(d).wait_send()
    for i in range(chunks):
        x_copy(i).wait_send()


def local(elementals, slice_scale, source_times, perambulators):
    half, modes = elementals.shape[1:3]
    slots = perambulators.shape[1]
    chunks, span = modes // CHUNK, half // PIECES
    dma, in_hbm = pltpu.SemaphoreType.DMA, pl.BlockSpec(memory_space=pltpu.HBM)
    return pl.pallas_call(
        kernel,
        out_shape=jax.ShapeDtypeStruct((1, slots, 2), F32),
        in_specs=[
            in_hbm,
            pl.BlockSpec(memory_space=pltpu.SMEM),
            pl.BlockSpec(memory_space=pltpu.VMEM),
            in_hbm,
        ],
        out_specs=pl.BlockSpec(memory_space=pltpu.VMEM),
        scratch_shapes=[
            pltpu.VMEM((half, modes, modes), BF16),
            pltpu.VMEM((chunks, half, CHUNK, modes), BF16),
            pltpu.VMEM((modes // 2, 2 * half, 2 * modes), BF16),
            pltpu.VMEM((2, half, modes, modes), BF16),
            pltpu.VMEM((2, slots, modes, modes), BF16),
            pltpu.VMEM((2, PIECES, slots * span, modes), BF16),
            pltpu.VMEM((2 * slots, 2 * modes, 2 * modes), BF16),
            pltpu.VMEM((4, CHUNK // 2, slots * span, 2 * modes), BF16),
            pltpu.VMEM((4, slots * CHUNK, span * modes), BF16),
            pltpu.VMEM((2, slots * CHUNK, modes), F32),
            pltpu.VMEM((slots, modes), F32),
            pltpu.VMEM((2, slots, modes), F32),
            pltpu.VMEM((2, slots, modes), F32),
            pltpu.VMEM((3, slots, modes), F32),
            pltpu.VMEM((PIECES, span * STRIDE * 2 // lax.axis_size("tm"), modes, modes), BF16),
            dma, dma((2,)),
            dma((chunks,)), dma((chunks,)),
            dma((2, PIECES)), dma((2, PIECES)),
            dma, dma,
            dma((2,)), dma((2,)),
            dma((3,)), dma((3,)),
            dma((PIECES,)), dma((PIECES,)),
        ],
        compiler_params=pltpu.CompilerParams(
            collective_id=0, has_side_effects=True, vmem_limit_bytes=60 * 2**20
        ),
    )(elementals, slice_scale, source_times.T, perambulators)


def solution(mesh):
    in_specs = (P("tm", "mode", None, None), P("tm"), P(), P("tm", None, None, None, None))
    return jax.shard_map(
        local, mesh=mesh, in_specs=in_specs, out_specs=P("tm", None, None), check_vma=False
    )
```

```python
import functools
import math

import jax
import jax.numpy as jnp
from jax import lax
from jax.experimental import pallas as pl
from jax.experimental.pallas import tpu as pltpu
from jax.sharding import PartitionSpec as P

MESH = pl.DeviceIdType.MESH
F32, BF16 = jnp.float32, jnp.bfloat16
CHUNK = 16
PIECES = 2
STRIDE = 8


def kernel(
    elem, scale, listed, peram, out,
    x_own, x_peer, x_rows, y_raw, blocks, left, right, first, moved, acc,
    scale_own, scale_far, part, far, passing, passing_blocks,
    own_sem, peram_sem, x_send, x_recv, y_send, y_recv, p_send, p_recv, s_send, s_recv, o_send, o_recv, r_send, r_recv, b_send, b_recv,
):
    slices = lax.axis_size("tm")
    t, h = lax.axis_index("tm"), lax.axis_index("mode")
    core = lax.rem(t, 2)
    half, modes = elem.shape[1], elem.shape[2]
    slots = peram.shape[1]
    chunks, span = modes // CHUNK, half // PIECES
    other = 1 - h

    def at(step):
        return lax.rem(t + step + slices, slices)

    def send(src, dst, ssem, rsem, device):
        return pltpu.make_async_remote_copy(
            src_ref=src, dst_ref=dst, send_sem=ssem, recv_sem=rsem, device_id=device, device_id_type=MESH
        )

    def x_copy(i):
        rows = pl.ds(i * CHUNK, CHUNK)
        return send(elem.at[0, :, rows, :], x_peer.at[i], x_send.at[i], x_recv.at[i], (t, other))

    def y_copy(j, q, device):
        rows = pl.ds(q * span, span)
        return send(elem.at[0, rows], y_raw.at[j, rows], y_send.at[j, q], y_recv.at[j, q], device)

    def forward(q):
        rows = pl.ds(q * span, span)
        return send(y_raw.at[1, rows], y_raw.at[0, rows], y_send.at[0, q], y_recv.at[0, q], (at(1), h))

    def peram_copy():
        return send(peram.at[0, :, 1], blocks.at[1], p_send, p_recv, (at(2), h))

    def scale_copy(d):
        return send(scale_own, scale_far.at[d], s_send.at[d], s_recv.at[d], (at(-1 - d), h))

    run = slices // 2
    place, upper = lax.rem(t, run), t // run
    relays = run // STRIDE
    share = span // relays
    rank = place // STRIDE
    lead = jnp.where(core == 1, 1, STRIDE - 2)
    at_source = place == jnp.where(core == 1, run - 1, 0)
    at_sink = place == jnp.where(core == 1, 1, run - 2)
    is_relay = (lax.rem(place, STRIDE) == lead) & jnp.logical_not(at_sink)
    sink = upper * run + jnp.where(core == 1, 1, run - 2)
    source = lax.rem(sink + jnp.where(core == 1, slices - 2, 2), slices)
    ahead = lax.rem(t + jnp.where(core == 1, 2, slices - 2), slices)

    def share_rows(q, k):
        return pl.ds(q * span + k * share, share)

    def share_copy(q, k, dst, rsem, device):
        return send(elem.at[0, share_rows(q, k)], dst, y_send.at[1, q], rsem, device)

    def pass_on(q):
        return send(passing.at[q], y_raw.at[1, share_rows(q, rank)], r_send.at[q], y_recv.at[1, q], (sink, h))

    held = slots // relays

    def block_copy(k, dst, rsem, device):
        return send(peram.at[0, pl.ds(k * held, held), 1], dst, p_send, rsem, device)

    def pass_blocks():
        return send(passing_blocks, blocks.at[1, pl.ds(rank * held, held)], b_send, p_recv, (sink, h))

    own_copy = pltpu.make_async_copy(elem.at[0], x_own, own_sem)
    own_copy.start()
    block_copies = [pltpu.make_async_copy(peram.at[0, :, d], blocks.at[d], peram_sem.at[d]) for d in range(2)]
    block_copies[0].start()

    @pl.when(core == 0)
    def _():
        block_copies[1].start()

    scale_own[...] = jnp.full(scale_own.shape, scale[0], F32)
    acc[...] = jnp.zeros_like(acc)

    barrier = pltpu.get_barrier_semaphore()
    near = [(t, other)] + [(at(k), h) for k in (-2, -1, 1, 2)] + [(at(k), other) for k in (-2, 2)]
    for device in near:
        pl.semaphore_signal(barrier, inc=1, device_id=device, device_id_type=MESH)

    @pl.when(is_relay)
    def _():
        pl.semaphore_signal(barrier, inc=1, device_id=(source, h), device_id_type=MESH)

    @pl.when(at_sink)
    def _():
        def greet(n, _):
            relay = upper * run + n * STRIDE + lead

            @pl.when(relay != t)
            def _():
                pl.semaphore_signal(barrier, inc=1, device_id=(relay, h), device_id_type=MESH)

            return 0

        lax.fori_loop(0, relays, greet, 0)

    further = jnp.where(is_relay, 1, 0) + jnp.where(at_source, relays - 1, 0)
    pl.semaphore_wait(barrier, len(near) + further)

    @pl.when(jnp.logical_not(at_source))
    def _():
        for i in range(2):
            x_copy(i).start()

    @pl.when((core == 1) & jnp.logical_not(at_source))
    def _():
        peram_copy().start()

    @pl.when((core == 1) & at_source)
    def _():
        def spread_blocks(k, _):
            relay = (1 - upper) * run + k * STRIDE + lead

            @pl.when(relay == ahead)
            def _():
                block_copy(k, blocks.at[1, pl.ds(k * held, held)], p_recv, (relay, h)).start()

            @pl.when(relay != ahead)
            def _():
                block_copy(k, passing_blocks, b_recv, (relay, h)).start()

            return 0

        lax.fori_loop(0, relays, spread_blocks, 0)

    @pl.when(at_source)
    def _():
        def spread(n, _):
            q, k = n // relays, lax.rem(n, relays)
            relay = (1 - upper) * run + k * STRIDE + lead

            @pl.when(relay == ahead)
            def _():
                share_copy(q, k, y_raw.at[1, share_rows(q, k)], y_recv.at[1, q], (relay, h)).start()

            @pl.when(relay != ahead)
            def _():
                share_copy(q, k, passing.at[q], r_recv.at[q], (relay, h)).start()

            return 0

        lax.fori_loop(0, relays, spread, 0)
        for g in range(2):
            x_copy(g).start()
        for g in range(2):
            lax.fori_loop((2 + g) * relays // 2, (3 + g) * relays // 2, spread, 0)
            x_copy(2 + 2 * g).start()
            x_copy(3 + 2 * g).start()

    @pl.when(jnp.logical_not(at_source))
    def _():
        for q in range(PIECES):
            y_copy(1, q, (ahead, h)).start()
        for g in range(2 * PIECES):
            x_copy(2 + g).start()

    @pl.when(core == 1)
    def _():
        for q in range(PIECES):
            y_copy(0, q, (at(-1), h)).start()

    for i in range(2 + 2 * PIECES, chunks):
        x_copy(i).start()
    for d in range(2):
        scale_copy(d).start()

    right[...] = jnp.zeros_like(right)
    own_rows = pl.multiple_of(h * half, half)

    def lay_blocks(j):
        swap = (core == 1) & (j == 1)

        def lay_block(r, _):
            block = blocks[j, r]
            turned = block.T
            row_form = jnp.where(swap, turned, block) if j else block
            column_form = jnp.where(swap, block, turned) if j else turned
            blocks[j, r] = row_form
            for q in range(PIECES):
                rows = pl.ds(pl.multiple_of(r * span, span), span)
                left[j, q, rows, :] = blocks[j, r, pl.ds(own_rows + q * span, span), :]
            right[j * slots + r, :modes, :modes] = column_form
            right[j * slots + r, modes:, modes:] = column_form
            return 0

        lax.fori_loop(0, slots, lay_block, 0)

    def lay_rows(chunk_rows, i, offset):
        turned = jnp.swapaxes(chunk_rows.astype(F32), 0, 1).astype(BF16)
        for p in range(CHUNK // 2):
            pair = jnp.concatenate([turned[p], turned[p + CHUNK // 2]], axis=1)
            x_rows[i * (CHUNK // 2) + p, pl.ds(offset, half), :] = pair

    def lay_own(i, _):
        rows = pl.ds(pl.multiple_of(i * CHUNK, CHUNK), CHUNK)
        lay_rows(x_own[:, rows, :], i, own_rows)
        return 0

    def relay_blocks():
        @pl.when((core == 1) & is_relay)
        def _():
            block_copy(0, passing_blocks, b_recv, (source, h)).wait_recv()
            pass_blocks().start()

    block_copies[0].wait()
    lay_blocks(0)
    own_copy.wait()
    lax.fori_loop(0, chunks, lay_own, 0)

    @pl.when(core == 0)
    def _():
        block_copies[1].wait()

    relay_blocks()

    @pl.when(core == 1)
    def _():
        peram_copy().wait_recv()

    lay_blocks(1)

    def take_near(q):
        y_copy(0, q, (at(-1), h)).wait_recv()

    def take_far(q):
        y_copy(1, q, (at(2), h)).wait_recv()

        @pl.when(core == 0)
        def _():
            forward(q).start()

    def relay(q):
        @pl.when(is_relay)
        def _():
            share_copy(q, 0, passing.at[q], r_recv.at[q], (source, h)).wait_recv()
            pass_on(q).start()

    def take_chunk(i):
        x_copy(i).wait_recv()
        lay_rows(x_peer[i], i, pl.multiple_of(other * half, half))

    near_late = (core == 1) & at_source
    far_late = (core == 1) & at_sink
    early = chunks // 2
    last = PIECES - 1

    def step(n, _):
        @pl.when(n == 0)
        def _():
            take_chunk(0)
            relay(0)
            take_far(0)
            take_near(0)
            take_chunk(1)

        @pl.when(n == 1)
        def _():
            take_chunk(2)
            relay(last)
            take_chunk(3)

        far_at = jnp.where(at_sink, jnp.where(core == 1, 3, 2), 1)

        @pl.when(n == far_at)
        def _():
            take_far(last)

        @pl.when(n == jnp.where(near_late, 3, 2))
        def _():
            take_near(last)

        @pl.when(n >= early)
        def _():
            take_chunk(n)

        pairs, apart = n < early, (near_late | far_late) & ((n == 2) | (n == 3))
        late_first = (n == 2) == near_late
        blocks_of = []
        for b in range(4):
            c = jnp.where(pairs, 2 * lax.rem(n, 2) + b // 2, n)
            q = jnp.where(pairs, n // 2, b // 2)
            c = jnp.where(apart, b, c)
            j = jnp.where(apart, jnp.where(late_first, 1, 0), b % 2)
            blocks_of.append((c, j, q))
        for b, (c, j, q) in enumerate(blocks_of):
            for p in range(CHUNK // 2):
                product = jnp.dot(left[j, q], x_rows[c * (CHUNK // 2) + p], preferred_element_type=F32)
                first[b, p] = product.astype(BF16)
        for b, (c, j, q) in enumerate(blocks_of):
            for r in range(slots):
                lhs = first[b, :, r * span:(r + 1) * span, :].reshape(CHUNK // 2 * span, 2 * modes)
                image = jnp.dot(lhs, right[j * slots + r], preferred_element_type=F32)
                turned = jnp.swapaxes(image.reshape(CHUNK // 2, span, 2 * modes), 0, 1)
                for y in range(span):
                    tile = jnp.concatenate([turned[y, :, :modes], turned[y, :, modes:]], axis=0)
                    moved[b, r * CHUNK:(r + 1) * CHUNK, y * modes:(y + 1) * modes] = tile.astype(BF16)
        for b, (c, j, q) in enumerate(blocks_of):
            rows = pl.ds(pl.multiple_of(c * CHUNK, CHUNK), CHUNK)
            sink_rows = jnp.concatenate([y_raw[j, q * span + y] for y in range(span)], axis=1)
            sums = lax.dot_general(moved[b], sink_rows, (((1,), (1,)), ((), ())), preferred_element_type=F32)
            weights = right[pl.ds(j * slots, slots), rows, :modes].reshape(slots * CHUNK, modes)
            acc[j] += sums * weights.astype(F32)
        return 0

    lax.fori_loop(0, chunks, step, 0)

    for j in range(2):
        total = jnp.sum(acc[j].reshape(slots, CHUNK, modes), axis=1)
        part[j] = jnp.broadcast_to(jnp.sum(total, axis=1, keepdims=True), (slots, modes))

    def part_copy(j, slot, device):
        return send(part.at[j], far.at[slot], o_send.at[slot], o_recv.at[slot], device)

    part_copy(0, 0, (t, other)).start()

    @pl.when(core == 0)
    def _():
        part_copy(1, 2, (t, other)).start()
        far[1] = part[1]

    @pl.when(core == 1)
    def _():
        part_copy(1, 1, (at(-2), h)).start()
        part_copy(1, 2, (at(-2), other)).start()

    live = jnp.sum((listed[...] == t).astype(jnp.int32))
    slot_of = lax.broadcasted_iota(jnp.int32, (slots, modes), 0)
    lane = lax.broadcasted_iota(jnp.int32, (slots, modes), 1)
    for d in range(2):
        scale_copy(d).wait_recv()
    factor = 1.0 / (modes * math.sqrt(modes))
    signs = [jnp.where(t + d >= slices, -factor, factor) for d in (1, 2)]
    weights = jnp.where(lane == 0, scale_far[0] * signs[0], scale_far[1] * signs[1]) * scale_own[...]

    part_copy(0, 0, (t, other)).wait_recv()
    part_copy(1, 2, (t, other)).wait_recv()

    @pl.when(core == 1)
    def _():
        part_copy(1, 1, (at(-2), h)).wait_recv()

    values = jnp.where(lane == 0, part[0] + far[0], far[1] + far[2]) * weights
    values = jnp.where(slot_of < live, values, 0.0)
    out[0] = values[:, :2]

    part_copy(0, 0, (t, other)).wait_send()
    part_copy(1, 2, (t, other)).wait_send()

    for q in range(PIECES):
        y_copy(1, q, (ahead, h)).wait_send()

    @pl.when(core == 0)
    def _():
        for q in range(PIECES):
            forward(q).wait_send()

    @pl.when(core == 1)
    def _():
        peram_copy().wait_send()
        part_copy(1, 1, (at(-2), h)).wait_send()
        for q in range(PIECES):
            y_copy(0, q, (at(-1), h)).wait_send()

    @pl.when(is_relay)
    def _():
        for q in range(PIECES):
            pass_on(q).wait_send()

    @pl.when((core == 1) & is_relay)
    def _():
        pass_blocks().wait_send()

    for d in range(2):
        scale_copy(d).wait_send()
    for i in range(chunks):
        x_copy(i).wait_send()


def local(elementals, slice_scale, source_times, perambulators):
    half, modes = elementals.shape[1:3]
    slots = perambulators.shape[1]
    chunks, span = modes // CHUNK, half // PIECES
    dma, in_hbm = pltpu.SemaphoreType.DMA, pl.BlockSpec(memory_space=pltpu.HBM)
    return pl.pallas_call(
        kernel,
        out_shape=jax.ShapeDtypeStruct((1, slots, 2), F32),
        in_specs=[
            in_hbm,
            pl.BlockSpec(memory_space=pltpu.SMEM),
            pl.BlockSpec(memory_space=pltpu.VMEM),
            in_hbm,
        ],
        out_specs=pl.BlockSpec(memory_space=pltpu.VMEM),
        scratch_shapes=[
            pltpu.VMEM((half, modes, modes), BF16),
            pltpu.VMEM((chunks, half, CHUNK, modes), BF16),
            pltpu.VMEM((modes // 2, 2 * half, 2 * modes), BF16),
            pltpu.VMEM((2, half, modes, modes), BF16),
            pltpu.VMEM((2, slots, modes, modes), BF16),
            pltpu.VMEM((2, PIECES, slots * span, modes), BF16),
            pltpu.VMEM((2 * slots, 2 * modes, 2 * modes), BF16),
            pltpu.VMEM((4, CHUNK // 2, slots * span, 2 * modes), BF16),
            pltpu.VMEM((4, slots * CHUNK, span * modes), BF16),
            pltpu.VMEM((2, slots * CHUNK, modes), F32),
            pltpu.VMEM((slots, modes), F32),
            pltpu.VMEM((2, slots, modes), F32),
            pltpu.VMEM((2, slots, modes), F32),
            pltpu.VMEM((3, slots, modes), F32),
            pltpu.VMEM((PIECES, span * STRIDE * 2 // lax.axis_size("tm"), modes, modes), BF16),
            pltpu.VMEM((slots * STRIDE * 2 // lax.axis_size("tm"), modes, modes), BF16),
            dma, dma((2,)),
            dma((chunks,)), dma((chunks,)),
            dma((2, PIECES)), dma((2, PIECES)),
            dma, dma,
            dma((2,)), dma((2,)),
            dma((3,)), dma((3,)),
            dma((PIECES,)), dma((PIECES,)),
            dma, dma,
        ],
        compiler_params=pltpu.CompilerParams(
            collective_id=0, has_side_effects=True, vmem_limit_bytes=60 * 2**20
        ),
    )(elementals, slice_scale, source_times.T, perambulators)


def solution(mesh):
    in_specs = (P("tm", "mode", None, None), P("tm"), P(), P("tm", None, None, None, None))
    return jax.shard_map(
        local, mesh=mesh, in_specs=in_specs, out_specs=P("tm", None, None), check_vma=False
    )
```

```python
import functools
import math

import jax
import jax.numpy as jnp
from jax import lax
from jax.experimental import pallas as pl
from jax.experimental.pallas import tpu as pltpu
from jax.sharding import PartitionSpec as P

MESH = pl.DeviceIdType.MESH
F32, BF16 = jnp.float32, jnp.bfloat16
CHUNK = 16
PIECES = 2
STRIDE = 8


def kernel(
    elem, scale, listed, peram, out,
    x_own, x_peer, x_rows, y_raw, blocks, left, right, first, moved, acc,
    scale_own, scale_far, part, far, passing, passing_blocks,
    own_sem, peram_sem, x_send, x_recv, y_send, y_recv, p_send, p_recv, s_send, s_recv, o_send, o_recv, r_send, r_recv, b_send, b_recv,
):
    slices = lax.axis_size("tm")
    t, h = lax.axis_index("tm"), lax.axis_index("mode")
    core = lax.rem(t, 2)
    half, modes = elem.shape[1], elem.shape[2]
    slots = peram.shape[1]
    chunks, span = modes // CHUNK, half // PIECES
    other = 1 - h

    def at(step):
        return lax.rem(t + step + slices, slices)

    def send(src, dst, ssem, rsem, device):
        return pltpu.make_async_remote_copy(
            src_ref=src, dst_ref=dst, send_sem=ssem, recv_sem=rsem, device_id=device, device_id_type=MESH
        )

    def x_copy(i):
        rows = pl.ds(i * CHUNK, CHUNK)
        return send(elem.at[0, :, rows, :], x_peer.at[i], x_send.at[i], x_recv.at[i], (t, other))

    def y_copy(j, q, device):
        rows = pl.ds(q * span, span)
        return send(elem.at[0, rows], y_raw.at[j, rows], y_send.at[j, q], y_recv.at[j, q], device)

    def forward(q):
        rows = pl.ds(q * span, span)
        return send(y_raw.at[1, rows], y_raw.at[0, rows], y_send.at[0, q], y_recv.at[0, q], (at(1), h))

    def peram_copy():
        return send(peram.at[0, :, 1], blocks.at[1], p_send, p_recv, (at(2), h))

    def scale_copy(d):
        return send(scale_own, scale_far.at[d], s_send.at[d], s_recv.at[d], (at(-1 - d), h))

    run = slices // 2
    place, upper = lax.rem(t, run), t // run
    relays = run // STRIDE
    share = span // relays
    rank = place // STRIDE
    lead = jnp.where(core == 1, 1, STRIDE - 2)
    at_source = place == jnp.where(core == 1, run - 1, 0)
    at_sink = place == jnp.where(core == 1, 1, run - 2)
    is_relay = (lax.rem(place, STRIDE) == lead) & jnp.logical_not(at_sink)
    sink = upper * run + jnp.where(core == 1, 1, run - 2)
    source = lax.rem(sink + jnp.where(core == 1, slices - 2, 2), slices)
    ahead = lax.rem(t + jnp.where(core == 1, 2, slices - 2), slices)

    def share_rows(q, k):
        return pl.ds(q * span + k * share, share)

    def share_copy(q, k, dst, rsem, device):
        return send(elem.at[0, share_rows(q, k)], dst, y_send.at[1, q], rsem, device)

    def pass_on(q):
        return send(passing.at[q], y_raw.at[1, share_rows(q, rank)], r_send.at[q], y_recv.at[1, q], (sink, h))

    held = slots // relays

    def block_copy(k, dst, rsem, device):
        return send(peram.at[0, pl.ds(k * held, held), 1], dst, p_send, rsem, device)

    def pass_blocks():
        return send(passing_blocks, blocks.at[1, pl.ds(rank * held, held)], b_send, p_recv, (sink, h))

    own_copy = pltpu.make_async_copy(elem.at[0], x_own, own_sem)
    own_copy.start()
    block_copies = [pltpu.make_async_copy(peram.at[0, :, d], blocks.at[d], peram_sem.at[d]) for d in range(2)]
    block_copies[0].start()

    @pl.when(core == 0)
    def _():
        block_copies[1].start()

    scale_own[...] = jnp.full(scale_own.shape, scale[0], F32)
    acc[...] = jnp.zeros_like(acc)

    barrier = pltpu.get_barrier_semaphore()
    near = [(t, other)] + [(at(k), h) for k in (-2, -1, 1, 2)] + [(at(k), other) for k in (-2, 2)]
    for device in near:
        pl.semaphore_signal(barrier, inc=1, device_id=device, device_id_type=MESH)

    @pl.when(is_relay)
    def _():
        pl.semaphore_signal(barrier, inc=1, device_id=(source, h), device_id_type=MESH)

    @pl.when(at_sink)
    def _():
        def greet(n, _):
            relay = upper * run + n * STRIDE + lead

            @pl.when(relay != t)
            def _():
                pl.semaphore_signal(barrier, inc=1, device_id=(relay, h), device_id_type=MESH)

            return 0

        lax.fori_loop(0, relays, greet, 0)

    further = jnp.where(is_relay, 1, 0) + jnp.where(at_source, relays - 1, 0)
    pl.semaphore_wait(barrier, len(near) + further)

    @pl.when(jnp.logical_not(at_source))
    def _():
        for i in range(2):
            x_copy(i).start()

    @pl.when((core == 1) & jnp.logical_not(at_source))
    def _():
        peram_copy().start()

    @pl.when((core == 1) & at_source)
    def _():
        def spread_blocks(k, _):
            relay = (1 - upper) * run + k * STRIDE + lead

            @pl.when(relay == ahead)
            def _():
                block_copy(k, blocks.at[1, pl.ds(k * held, held)], p_recv, (relay, h)).start()

            @pl.when(relay != ahead)
            def _():
                block_copy(k, passing_blocks, b_recv, (relay, h)).start()

            return 0

        lax.fori_loop(0, relays, spread_blocks, 0)

    @pl.when(at_source)
    def _():
        def spread(n, _):
            q, k = n // relays, lax.rem(n, relays)
            relay = (1 - upper) * run + k * STRIDE + lead

            @pl.when(relay == ahead)
            def _():
                share_copy(q, k, y_raw.at[1, share_rows(q, k)], y_recv.at[1, q], (relay, h)).start()

            @pl.when(relay != ahead)
            def _():
                share_copy(q, k, passing.at[q], r_recv.at[q], (relay, h)).start()

            return 0

        lax.fori_loop(0, relays, spread, 0)
        for g in range(2):
            x_copy(g).start()
        for g in range(2):
            lax.fori_loop((2 + g) * relays // 2, (3 + g) * relays // 2, spread, 0)
            x_copy(2 + 2 * g).start()
            x_copy(3 + 2 * g).start()

    @pl.when(jnp.logical_not(at_source))
    def _():
        for q in range(PIECES):
            y_copy(1, q, (ahead, h)).start()
        for g in range(2 * PIECES):
            x_copy(2 + g).start()

    @pl.when(core == 1)
    def _():
        for q in range(PIECES):
            y_copy(0, q, (at(-1), h)).start()

    for i in range(2 + 2 * PIECES, chunks):
        x_copy(i).start()
    for d in range(2):
        scale_copy(d).start()

    right[...] = jnp.zeros_like(right)
    own_rows = pl.multiple_of(h * half, half)

    def lay_blocks(j):
        swap = (core == 1) & (j == 1)

        def lay_block(r, _):
            block = blocks[j, r]
            turned = block.T
            row_form = jnp.where(swap, turned, block) if j else block
            column_form = jnp.where(swap, block, turned) if j else turned
            blocks[j, r] = row_form
            for q in range(PIECES):
                rows = pl.ds(pl.multiple_of(r * span, span), span)
                left[j, q, rows, :] = blocks[j, r, pl.ds(own_rows + q * span, span), :]
            right[j * slots + r, :modes, :modes] = column_form
            right[j * slots + r, modes:, modes:] = column_form
            return 0

        lax.fori_loop(0, slots, lay_block, 0)

    def lay_rows(chunk_rows, i, offset):
        turned = jnp.swapaxes(chunk_rows.astype(F32), 0, 1).astype(BF16)
        for p in range(CHUNK // 2):
            pair = jnp.concatenate([turned[p], turned[p + CHUNK // 2]], axis=1)
            x_rows[i * (CHUNK // 2) + p, pl.ds(offset, half), :] = pair

    def lay_own(i, _):
        rows = pl.ds(pl.multiple_of(i * CHUNK, CHUNK), CHUNK)
        lay_rows(x_own[:, rows, :], i, own_rows)
        return 0

    def relay_blocks():
        @pl.when((core == 1) & is_relay)
        def _():
            block_copy(0, passing_blocks, b_recv, (source, h)).wait_recv()
            pass_blocks().start()

    block_copies[0].wait()
    lay_blocks(0)
    own_copy.wait()
    lax.fori_loop(0, chunks, lay_own, 0)

    @pl.when(core == 0)
    def _():
        block_copies[1].wait()

    relay_blocks()

    @pl.when(core == 1)
    def _():
        peram_copy().wait_recv()

    lay_blocks(1)

    def take_near(q):
        y_copy(0, q, (at(-1), h)).wait_recv()

    def take_far(q):
        y_copy(1, q, (at(2), h)).wait_recv()

        @pl.when(core == 0)
        def _():
            forward(q).start()

    def relay(q):
        @pl.when(is_relay)
        def _():
            share_copy(q, 0, passing.at[q], r_recv.at[q], (source, h)).wait_recv()
            pass_on(q).start()

    def take_chunk(i):
        x_copy(i).wait_recv()
        lay_rows(x_peer[i], i, pl.multiple_of(other * half, half))

    near_late = (core == 1) & (at_source | (place == STRIDE - 1))
    far_late = (core == 1) & (at_sink | (place == run - STRIDE + 1))
    row_end = lax.rem(place, STRIDE) == STRIDE - 2
    early = chunks // 2
    last = PIECES - 1

    def step(n, _):
        @pl.when(n == 0)
        def _():
            take_chunk(0)
            relay(0)
            take_far(0)
            take_near(0)
            take_chunk(1)

        @pl.when(n == 1)
        def _():
            take_chunk(2)
            relay(last)
            take_chunk(3)

        far_at = jnp.where(core == 1, jnp.where(far_late, 3, 2), jnp.where(row_end, 2, 1))

        @pl.when(n == far_at)
        def _():
            take_far(last)

        @pl.when(n == jnp.where(near_late, 3, 2))
        def _():
            take_near(last)

        @pl.when(n >= early)
        def _():
            take_chunk(n)

        pairs, apart = n < early, (near_late | far_late) & ((n == 2) | (n == 3))
        late_first = (n == 2) == near_late
        blocks_of = []
        for b in range(4):
            c = jnp.where(pairs, 2 * lax.rem(n, 2) + b // 2, n)
            q = jnp.where(pairs, n // 2, b // 2)
            c = jnp.where(apart, b, c)
            j = jnp.where(apart, jnp.where(late_first, 1, 0), b % 2)
            blocks_of.append((c, j, q))
        for b, (c, j, q) in enumerate(blocks_of):
            for p in range(CHUNK // 2):
                product = jnp.dot(left[j, q], x_rows[c * (CHUNK // 2) + p], preferred_element_type=F32)
                first[b, p] = product.astype(BF16)
        for b, (c, j, q) in enumerate(blocks_of):
            for r in range(slots):
                lhs = first[b, :, r * span:(r + 1) * span, :].reshape(CHUNK // 2 * span, 2 * modes)
                image = jnp.dot(lhs, right[j * slots + r], preferred_element_type=F32)
                turned = jnp.swapaxes(image.reshape(CHUNK // 2, span, 2 * modes), 0, 1)
                for y in range(span):
                    tile = jnp.concatenate([turned[y, :, :modes], turned[y, :, modes:]], axis=0)
                    moved[b, r * CHUNK:(r + 1) * CHUNK, y * modes:(y + 1) * modes] = tile.astype(BF16)
        for b, (c, j, q) in enumerate(blocks_of):
            rows = pl.ds(pl.multiple_of(c * CHUNK, CHUNK), CHUNK)
            sink_rows = jnp.concatenate([y_raw[j, q * span + y] for y in range(span)], axis=1)
            sums = lax.dot_general(moved[b], sink_rows, (((1,), (1,)), ((), ())), preferred_element_type=F32)
            weights = right[pl.ds(j * slots, slots), rows, :modes].reshape(slots * CHUNK, modes)
            acc[j] += sums * weights.astype(F32)
        return 0

    lax.fori_loop(0, chunks, step, 0)

    for j in range(2):
        total = jnp.sum(acc[j].reshape(slots, CHUNK, modes), axis=1)
        part[j] = jnp.broadcast_to(jnp.sum(total, axis=1, keepdims=True), (slots, modes))

    def part_copy(j, slot, device):
        return send(part.at[j], far.at[slot], o_send.at[slot], o_recv.at[slot], device)

    part_copy(0, 0, (t, other)).start()

    @pl.when(core == 0)
    def _():
        part_copy(1, 2, (t, other)).start()
        far[1] = part[1]

    @pl.when(core == 1)
    def _():
        part_copy(1, 1, (at(-2), h)).start()
        part_copy(1, 2, (at(-2), other)).start()

    live = jnp.sum((listed[...] == t).astype(jnp.int32))
    slot_of = lax.broadcasted_iota(jnp.int32, (slots, modes), 0)
    lane = lax.broadcasted_iota(jnp.int32, (slots, modes), 1)
    for d in range(2):
        scale_copy(d).wait_recv()
    factor = 1.0 / (modes * math.sqrt(modes))
    signs = [jnp.where(t + d >= slices, -factor, factor) for d in (1, 2)]
    weights = jnp.where(lane == 0, scale_far[0] * signs[0], scale_far[1] * signs[1]) * scale_own[...]

    part_copy(0, 0, (t, other)).wait_recv()
    part_copy(1, 2, (t, other)).wait_recv()

    @pl.when(core == 1)
    def _():
        part_copy(1, 1, (at(-2), h)).wait_recv()

    values = jnp.where(lane == 0, part[0] + far[0], far[1] + far[2]) * weights
    values = jnp.where(slot_of < live, values, 0.0)
    out[0] = values[:, :2]

    part_copy(0, 0, (t, other)).wait_send()
    part_copy(1, 2, (t, other)).wait_send()

    for q in range(PIECES):
        y_copy(1, q, (ahead, h)).wait_send()

    @pl.when(core == 0)
    def _():
        for q in range(PIECES):
            forward(q).wait_send()

    @pl.when(core == 1)
    def _():
        peram_copy().wait_send()
        part_copy(1, 1, (at(-2), h)).wait_send()
        for q in range(PIECES):
            y_copy(0, q, (at(-1), h)).wait_send()

    @pl.when(is_relay)
    def _():
        for q in range(PIECES):
            pass_on(q).wait_send()

    @pl.when((core == 1) & is_relay)
    def _():
        pass_blocks().wait_send()

    for d in range(2):
        scale_copy(d).wait_send()
    for i in range(chunks):
        x_copy(i).wait_send()


def local(elementals, slice_scale, source_times, perambulators):
    half, modes = elementals.shape[1:3]
    slots = perambulators.shape[1]
    chunks, span = modes // CHUNK, half // PIECES
    dma, in_hbm = pltpu.SemaphoreType.DMA, pl.BlockSpec(memory_space=pltpu.HBM)
    return pl.pallas_call(
        kernel,
        out_shape=jax.ShapeDtypeStruct((1, slots, 2), F32),
        in_specs=[
            in_hbm,
            pl.BlockSpec(memory_space=pltpu.SMEM),
            pl.BlockSpec(memory_space=pltpu.VMEM),
            in_hbm,
        ],
        out_specs=pl.BlockSpec(memory_space=pltpu.VMEM),
        scratch_shapes=[
            pltpu.VMEM((half, modes, modes), BF16),
            pltpu.VMEM((chunks, half, CHUNK, modes), BF16),
            pltpu.VMEM((modes // 2, 2 * half, 2 * modes), BF16),
            pltpu.VMEM((2, half, modes, modes), BF16),
            pltpu.VMEM((2, slots, modes, modes), BF16),
            pltpu.VMEM((2, PIECES, slots * span, modes), BF16),
            pltpu.VMEM((2 * slots, 2 * modes, 2 * modes), BF16),
            pltpu.VMEM((4, CHUNK // 2, slots * span, 2 * modes), BF16),
            pltpu.VMEM((4, slots * CHUNK, span * modes), BF16),
            pltpu.VMEM((2, slots * CHUNK, modes), F32),
            pltpu.VMEM((slots, modes), F32),
            pltpu.VMEM((2, slots, modes), F32),
            pltpu.VMEM((2, slots, modes), F32),
            pltpu.VMEM((3, slots, modes), F32),
            pltpu.VMEM((PIECES, span * STRIDE * 2 // lax.axis_size("tm"), modes, modes), BF16),
            pltpu.VMEM((slots * STRIDE * 2 // lax.axis_size("tm"), modes, modes), BF16),
            dma, dma((2,)),
            dma((chunks,)), dma((chunks,)),
            dma((2, PIECES)), dma((2, PIECES)),
            dma, dma,
            dma((2,)), dma((2,)),
            dma((3,)), dma((3,)),
            dma((PIECES,)), dma((PIECES,)),
            dma, dma,
        ],
        compiler_params=pltpu.CompilerParams(
            collective_id=0, has_side_effects=True, vmem_limit_bytes=60 * 2**20
        ),
    )(elementals, slice_scale, source_times.T, perambulators)


def solution(mesh):
    in_specs = (P("tm", "mode", None, None), P("tm"), P(), P("tm", None, None, None, None))
    return jax.shard_map(
        local, mesh=mesh, in_specs=in_specs, out_specs=P("tm", None, None), check_vma=False
    )
```

```python
import functools
import math

import jax
import jax.numpy as jnp
from jax import lax
from jax.experimental import pallas as pl
from jax.experimental.pallas import tpu as pltpu
from jax.sharding import PartitionSpec as P

MESH = pl.DeviceIdType.MESH
F32, BF16 = jnp.float32, jnp.bfloat16
CHUNK = 16
PIECES = 2
STRIDE = 8


def kernel(
    elem, scale, listed, peram, out,
    x_own, x_peer, x_rows, y_raw, blocks, left, right, first, moved, acc,
    scale_own, scale_far, part, far, passing, passing_blocks,
    own_sem, peram_sem, x_send, x_recv, y_send, y_recv, p_send, p_recv, s_send, s_recv, o_send, o_recv, r_send, r_recv, b_send, b_recv,
):
    slices = lax.axis_size("tm")
    t, h = lax.axis_index("tm"), lax.axis_index("mode")
    core = lax.rem(t, 2)
    half, modes = elem.shape[1], elem.shape[2]
    slots = peram.shape[1]
    chunks, span = modes // CHUNK, half // PIECES
    other = 1 - h

    def at(step):
        return lax.rem(t + step + slices, slices)

    def send(src, dst, ssem, rsem, device):
        return pltpu.make_async_remote_copy(
            src_ref=src, dst_ref=dst, send_sem=ssem, recv_sem=rsem, device_id=device, device_id_type=MESH
        )

    def x_copy(i):
        rows = pl.ds(i * CHUNK, CHUNK)
        return send(elem.at[0, :, rows, :], x_peer.at[i], x_send.at[i], x_recv.at[i], (t, other))

    def y_copy(j, q, device):
        rows = pl.ds(q * span, span)
        return send(elem.at[0, rows], y_raw.at[j, rows], y_send.at[j, q], y_recv.at[j, q], device)

    def forward(q):
        rows = pl.ds(q * span, span)
        return send(y_raw.at[1, rows], y_raw.at[0, rows], y_send.at[0, q], y_recv.at[0, q], (at(1), h))

    def peram_copy():
        return send(peram.at[0, :, 1], blocks.at[1], p_send, p_recv, (at(2), h))

    def scale_copy(d):
        return send(scale_own, scale_far.at[d], s_send.at[d], s_recv.at[d], (at(-1 - d), h))

    run = slices // 2
    place, upper = lax.rem(t, run), t // run
    relays = run // STRIDE
    share = span // relays
    rank = place // STRIDE
    lead = jnp.where(core == 1, 1, STRIDE - 2)
    at_source = place == jnp.where(core == 1, run - 1, 0)
    at_sink = place == jnp.where(core == 1, 1, run - 2)
    is_relay = (lax.rem(place, STRIDE) == lead) & jnp.logical_not(at_sink)
    sink = upper * run + jnp.where(core == 1, 1, run - 2)
    source = lax.rem(sink + jnp.where(core == 1, slices - 2, 2), slices)
    ahead = lax.rem(t + jnp.where(core == 1, 2, slices - 2), slices)

    def share_rows(q, k):
        return pl.ds(q * span + k * share, share)

    def share_copy(q, k, dst, rsem, device):
        return send(elem.at[0, share_rows(q, k)], dst, y_send.at[1, q], rsem, device)

    def pass_on(q):
        return send(passing.at[q], y_raw.at[1, share_rows(q, rank)], r_send.at[q], y_recv.at[1, q], (sink, h))

    held = slots // relays

    def block_copy(k, dst, rsem, device):
        return send(peram.at[0, pl.ds(k * held, held), 1], dst, p_send, rsem, device)

    def pass_blocks():
        return send(passing_blocks, blocks.at[1, pl.ds(rank * held, held)], b_send, p_recv, (sink, h))

    own_copy = pltpu.make_async_copy(elem.at[0], x_own, own_sem)
    own_copy.start()
    block_copies = [pltpu.make_async_copy(peram.at[0, :, d], blocks.at[d], peram_sem.at[d]) for d in range(2)]
    block_copies[0].start()

    @pl.when(core == 0)
    def _():
        block_copies[1].start()

    scale_own[...] = jnp.full(scale_own.shape, scale[0], F32)
    acc[...] = jnp.zeros_like(acc)

    barrier = pltpu.get_barrier_semaphore()
    near = [(t, other)] + [(at(k), h) for k in (-2, -1, 1, 2)] + [(at(k), other) for k in (-2, 2)]
    for device in near:
        pl.semaphore_signal(barrier, inc=1, device_id=device, device_id_type=MESH)

    @pl.when(is_relay)
    def _():
        pl.semaphore_signal(barrier, inc=1, device_id=(source, h), device_id_type=MESH)

    @pl.when(at_sink)
    def _():
        def greet(n, _):
            relay = upper * run + n * STRIDE + lead

            @pl.when(relay != t)
            def _():
                pl.semaphore_signal(barrier, inc=1, device_id=(relay, h), device_id_type=MESH)

            return 0

        lax.fori_loop(0, relays, greet, 0)

    further = jnp.where(is_relay, 1, 0) + jnp.where(at_source, relays - 1, 0)
    pl.semaphore_wait(barrier, len(near) + further)

    @pl.when(jnp.logical_not(at_source))
    def _():
        for i in range(2):
            x_copy(i).start()

    @pl.when((core == 1) & jnp.logical_not(at_source))
    def _():
        peram_copy().start()

    @pl.when((core == 1) & at_source)
    def _():
        def spread_blocks(k, _):
            relay = (1 - upper) * run + k * STRIDE + lead

            @pl.when(relay == ahead)
            def _():
                block_copy(k, blocks.at[1, pl.ds(k * held, held)], p_recv, (relay, h)).start()

            @pl.when(relay != ahead)
            def _():
                block_copy(k, passing_blocks, b_recv, (relay, h)).start()

            return 0

        lax.fori_loop(0, relays, spread_blocks, 0)

    @pl.when(at_source)
    def _():
        def spread(n, _):
            q, k = n // relays, lax.rem(n, relays)
            relay = (1 - upper) * run + k * STRIDE + lead

            @pl.when(relay == ahead)
            def _():
                share_copy(q, k, y_raw.at[1, share_rows(q, k)], y_recv.at[1, q], (relay, h)).start()

            @pl.when(relay != ahead)
            def _():
                share_copy(q, k, passing.at[q], r_recv.at[q], (relay, h)).start()

            return 0

        lax.fori_loop(0, relays, spread, 0)
        for g in range(2):
            x_copy(g).start()
        for g in range(2):
            lax.fori_loop((2 + g) * relays // 2, (3 + g) * relays // 2, spread, 0)
            x_copy(2 + 2 * g).start()
            x_copy(3 + 2 * g).start()

    @pl.when(jnp.logical_not(at_source))
    def _():
        for q in range(PIECES):
            y_copy(1, q, (ahead, h)).start()
        for g in range(2 * PIECES):
            x_copy(2 + g).start()

    @pl.when(core == 1)
    def _():
        for q in range(PIECES):
            y_copy(0, q, (at(-1), h)).start()

    for i in range(2 + 2 * PIECES, chunks):
        x_copy(i).start()
    for d in range(2):
        scale_copy(d).start()

    right[...] = jnp.zeros_like(right)
    own_rows = pl.multiple_of(h * half, half)

    def lay_blocks(j):
        swap = (core == 1) & (j == 1)

        def lay_block(r, _):
            block = blocks[j, r]
            turned = block.T
            row_form = jnp.where(swap, turned, block) if j else block
            column_form = jnp.where(swap, block, turned) if j else turned
            blocks[j, r] = row_form
            for q in range(PIECES):
                rows = pl.ds(pl.multiple_of(r * span, span), span)
                left[j, q, rows, :] = blocks[j, r, pl.ds(own_rows + q * span, span), :]
            right[j * slots + r, :modes, :modes] = column_form
            right[j * slots + r, modes:, modes:] = column_form
            return 0

        lax.fori_loop(0, slots, lay_block, 0)

    def lay_rows(chunk_rows, i, offset):
        turned = jnp.swapaxes(chunk_rows.astype(F32), 0, 1).astype(BF16)
        for p in range(CHUNK // 2):
            pair = jnp.concatenate([turned[p], turned[p + CHUNK // 2]], axis=1)
            x_rows[i * (CHUNK // 2) + p, pl.ds(offset, half), :] = pair

    def lay_own(i, _):
        rows = pl.ds(pl.multiple_of(i * CHUNK, CHUNK), CHUNK)
        lay_rows(x_own[:, rows, :], i, own_rows)
        return 0

    def relay_blocks():
        @pl.when((core == 1) & is_relay)
        def _():
            block_copy(0, passing_blocks, b_recv, (source, h)).wait_recv()
            pass_blocks().start()

    block_copies[0].wait()
    lay_blocks(0)
    own_copy.wait()
    lax.fori_loop(0, chunks, lay_own, 0)

    @pl.when(core == 0)
    def _():
        block_copies[1].wait()

    relay_blocks()

    @pl.when(core == 1)
    def _():
        peram_copy().wait_recv()

    lay_blocks(1)

    def take_near(q):
        y_copy(0, q, (at(-1), h)).wait_recv()

    def take_far(q):
        y_copy(1, q, (at(2), h)).wait_recv()

        @pl.when(core == 0)
        def _():
            forward(q).start()

    def relay(q):
        @pl.when(is_relay)
        def _():
            share_copy(q, 0, passing.at[q], r_recv.at[q], (source, h)).wait_recv()
            pass_on(q).start()

    def take_chunk(i):
        x_copy(i).wait_recv()
        lay_rows(x_peer[i], i, pl.multiple_of(other * half, half))

    near_late = (core == 1) & (lax.rem(place, STRIDE) == STRIDE - 1)
    far_late = (core == 1) & (at_sink | (place == run - STRIDE + 1))
    row_end = lax.rem(place, STRIDE) == STRIDE - 2
    early = chunks // 2
    last = PIECES - 1

    def step(n, _):
        @pl.when(n == 0)
        def _():
            take_chunk(0)
            relay(0)
            take_far(0)
            take_near(0)
            take_chunk(1)

        @pl.when(n == 1)
        def _():
            take_chunk(2)
            relay(last)
            take_chunk(3)

        far_at = jnp.where(core == 1, jnp.where(far_late, 3, 2), jnp.where(row_end, 2, 1))

        @pl.when(n == far_at)
        def _():
            take_far(last)

        @pl.when(n == jnp.where(near_late, 3, 2))
        def _():
            take_near(last)

        @pl.when(n >= early)
        def _():
            take_chunk(n)

        pairs, apart = n < early, (near_late | far_late) & ((n == 2) | (n == 3))
        late_first = (n == 2) == near_late
        blocks_of = []
        for b in range(4):
            c = jnp.where(pairs, 2 * lax.rem(n, 2) + b // 2, n)
            q = jnp.where(pairs, n // 2, b // 2)
            c = jnp.where(apart, b, c)
            j = jnp.where(apart, jnp.where(late_first, 1, 0), b % 2)
            blocks_of.append((c, j, q))
        for b, (c, j, q) in enumerate(blocks_of):
            for p in range(CHUNK // 2):
                product = jnp.dot(left[j, q], x_rows[c * (CHUNK // 2) + p], preferred_element_type=F32)
                first[b, p] = product.astype(BF16)
        for b, (c, j, q) in enumerate(blocks_of):
            for r in range(slots):
                lhs = first[b, :, r * span:(r + 1) * span, :].reshape(CHUNK // 2 * span, 2 * modes)
                image = jnp.dot(lhs, right[j * slots + r], preferred_element_type=F32)
                turned = jnp.swapaxes(image.reshape(CHUNK // 2, span, 2 * modes), 0, 1)
                for y in range(span):
                    tile = jnp.concatenate([turned[y, :, :modes], turned[y, :, modes:]], axis=0)
                    moved[b, r * CHUNK:(r + 1) * CHUNK, y * modes:(y + 1) * modes] = tile.astype(BF16)
        for b, (c, j, q) in enumerate(blocks_of):
            rows = pl.ds(pl.multiple_of(c * CHUNK, CHUNK), CHUNK)
            sink_rows = jnp.concatenate([y_raw[j, q * span + y] for y in range(span)], axis=1)
            sums = lax.dot_general(moved[b], sink_rows, (((1,), (1,)), ((), ())), preferred_element_type=F32)
            weights = right[pl.ds(j * slots, slots), rows, :modes].reshape(slots * CHUNK, modes)
            acc[j] += sums * weights.astype(F32)
        return 0

    lax.fori_loop(0, chunks, step, 0)

    for j in range(2):
        total = jnp.sum(acc[j].reshape(slots, CHUNK, modes), axis=1)
        part[j] = jnp.broadcast_to(jnp.sum(total, axis=1, keepdims=True), (slots, modes))

    def part_copy(j, slot, device):
        return send(part.at[j], far.at[slot], o_send.at[slot], o_recv.at[slot], device)

    part_copy(0, 0, (t, other)).start()

    @pl.when(core == 0)
    def _():
        part_copy(1, 2, (t, other)).start()
        far[1] = part[1]

    @pl.when(core == 1)
    def _():
        part_copy(1, 1, (at(-2), h)).start()
        part_copy(1, 2, (at(-2), other)).start()

    live = jnp.sum((listed[...] == t).astype(jnp.int32))
    slot_of = lax.broadcasted_iota(jnp.int32, (slots, modes), 0)
    lane = lax.broadcasted_iota(jnp.int32, (slots, modes), 1)
    for d in range(2):
        scale_copy(d).wait_recv()
    factor = 1.0 / (modes * math.sqrt(modes))
    signs = [jnp.where(t + d >= slices, -factor, factor) for d in (1, 2)]
    weights = jnp.where(lane == 0, scale_far[0] * signs[0], scale_far[1] * signs[1]) * scale_own[...]

    part_copy(0, 0, (t, other)).wait_recv()
    part_copy(1, 2, (t, other)).wait_recv()

    @pl.when(core == 1)
    def _():
        part_copy(1, 1, (at(-2), h)).wait_recv()

    values = jnp.where(lane == 0, part[0] + far[0], far[1] + far[2]) * weights
    values = jnp.where(slot_of < live, values, 0.0)
    out[0] = values[:, :2]

    part_copy(0, 0, (t, other)).wait_send()
    part_copy(1, 2, (t, other)).wait_send()

    for q in range(PIECES):
        y_copy(1, q, (ahead, h)).wait_send()

    @pl.when(core == 0)
    def _():
        for q in range(PIECES):
            forward(q).wait_send()

    @pl.when(core == 1)
    def _():
        peram_copy().wait_send()
        part_copy(1, 1, (at(-2), h)).wait_send()
        for q in range(PIECES):
            y_copy(0, q, (at(-1), h)).wait_send()

    @pl.when(is_relay)
    def _():
        for q in range(PIECES):
            pass_on(q).wait_send()

    @pl.when((core == 1) & is_relay)
    def _():
        pass_blocks().wait_send()

    for d in range(2):
        scale_copy(d).wait_send()
    for i in range(chunks):
        x_copy(i).wait_send()


def local(elementals, slice_scale, source_times, perambulators):
    half, modes = elementals.shape[1:3]
    slots = perambulators.shape[1]
    chunks, span = modes // CHUNK, half // PIECES
    dma, in_hbm = pltpu.SemaphoreType.DMA, pl.BlockSpec(memory_space=pltpu.HBM)
    return pl.pallas_call(
        kernel,
        out_shape=jax.ShapeDtypeStruct((1, slots, 2), F32),
        in_specs=[
            in_hbm,
            pl.BlockSpec(memory_space=pltpu.SMEM),
            pl.BlockSpec(memory_space=pltpu.VMEM),
            in_hbm,
        ],
        out_specs=pl.BlockSpec(memory_space=pltpu.VMEM),
        scratch_shapes=[
            pltpu.VMEM((half, modes, modes), BF16),
            pltpu.VMEM((chunks, half, CHUNK, modes), BF16),
            pltpu.VMEM((modes // 2, 2 * half, 2 * modes), BF16),
            pltpu.VMEM((2, half, modes, modes), BF16),
            pltpu.VMEM((2, slots, modes, modes), BF16),
            pltpu.VMEM((2, PIECES, slots * span, modes), BF16),
            pltpu.VMEM((2 * slots, 2 * modes, 2 * modes), BF16),
            pltpu.VMEM((4, CHUNK // 2, slots * span, 2 * modes), BF16),
            pltpu.VMEM((4, slots * CHUNK, span * modes), BF16),
            pltpu.VMEM((2, slots * CHUNK, modes), F32),
            pltpu.VMEM((slots, modes), F32),
            pltpu.VMEM((2, slots, modes), F32),
            pltpu.VMEM((2, slots, modes), F32),
            pltpu.VMEM((3, slots, modes), F32),
            pltpu.VMEM((PIECES, span * STRIDE * 2 // lax.axis_size("tm"), modes, modes), BF16),
            pltpu.VMEM((slots * STRIDE * 2 // lax.axis_size("tm"), modes, modes), BF16),
            dma, dma((2,)),
            dma((chunks,)), dma((chunks,)),
            dma((2, PIECES)), dma((2, PIECES)),
            dma, dma,
            dma((2,)), dma((2,)),
            dma((3,)), dma((3,)),
            dma((PIECES,)), dma((PIECES,)),
            dma, dma,
        ],
        compiler_params=pltpu.CompilerParams(
            collective_id=0, has_side_effects=True, vmem_limit_bytes=60 * 2**20
        ),
    )(elementals, slice_scale, source_times.T, perambulators)


def solution(mesh):
    in_specs = (P("tm", "mode", None, None), P("tm"), P(), P("tm", None, None, None, None))
    return jax.shard_map(
        local, mesh=mesh, in_specs=in_specs, out_specs=P("tm", None, None), check_vma=False
    )
```
